32 devices in a mesh: ctx: 16 (over z, x, core), head: 2 (over y).
Axes of the slice: x: 2, y: 2, z: 4, core: 2. Of those that a mesh axis runs over, the one named last changes fastest.
Arguments:
- queries: bfloat16 [3072, 4096], P('ctx', 'head'), may hold values from -6 to 6
- key_rows: bfloat16 [3072, 4096], P('ctx', 'head'), may hold values from -6 to 6
- value_rows: bfloat16 [3072, 4096], P('ctx', 'head'), may hold values from -120 to 120
- gate_rows: bfloat16 [3072, 4096], P('ctx', 'head'), may hold values from -8 to 8
- cotangent: bfloat16 [3072, 4096], P('ctx', 'head'), may hold values from -6 to 6
Outputs:
- grad_queries: bfloat16 [3072, 4096], P('ctx', 'head')
- grad_keys: bfloat16 [3072, 4096], P('ctx', 'head')
- grad_values: bfloat16 [3072, 4096], P('ctx', 'head')
- grad_gates: bfloat16 [3072, 4096], P('ctx', 'head')
The draws below stay inside these ranges and needn't reach their ends.
All inputs are finite; a program needn't handle non-finite values.
Results may differ from the reference program's by a relative error of at most 0.0065.
Values sent between devices are 32-bit elements; how exact they have to be, the bound alone decides.
No kernel may reach another device: no remote copies, remote signals or barrier semaphores. Data moves between devices by JAX's collectives and lax.ppermute only.
A program may use at most 64 MiB of HBM per device.

```python
import jax
import jax.numpy as jnp
from jax import lax

H = 32
DH = 128
TOK_DEV = 192
HD = 4096
TOKENS = 3072
N_CTX = 16


def draw_value_rows(key, part):
    first, second, third = jax.random.split(key, 3)
    width = H * DH
    row_scale = jnp.exp(jax.random.uniform(second, (TOKENS, 1), jnp.float32) * jnp.log(10.0))
    base = jnp.clip(jax.random.normal(first, (TOKENS, width), jnp.float32), -4.0, 4.0)
    jitter = jnp.exp(jax.random.uniform(third, (1, width), jnp.float32) * jnp.log(3.0))
    head_index = (jnp.arange(width) // DH).astype(jnp.float32)[None, :]
    ramp = jnp.exp(jnp.log(4.0) * head_index / (H - 1))
    col_scale = jitter * ramp
    return (base * row_scale * col_scale / 4.0).astype(jnp.bfloat16)


def block_scale(stream_key, shape, cuts, smallest, top_value):
    def one(axis_at, blocks):
        steps = jax.random.uniform(jax.random.fold_in(jax.random.fold_in(stream_key, 6), axis_at), (blocks,), jnp.float32, smallest / len(cuts), top_value / len(cuts))
        return jnp.repeat(jnp.exp(steps), shape[axis_at] // blocks).reshape((-1,) + (1,) * (len(shape) - axis_at - 1))

    loudness = one(*cuts[0])
    for cut in cuts[1:]:
        loudness = loudness * one(*cut)
    return loudness


def centred(stream_key, extent, scale, most, cuts=(), kind=jnp.bfloat16):
    factor_of = block_scale(stream_key, extent, cuts, -0.22, 0.18) if cuts else 1.0
    values = jax.random.normal(stream_key, extent, jnp.float32) * scale * factor_of
    return jnp.minimum(jnp.maximum(values, -most), most).astype(kind)


def setup_inputs(seed: int = 0) -> dict:
    key_list = jax.random.split(jax.random.key(seed), 6)
    queries = centred(key_list[0], (TOKENS, HD), 1.0, 6.0, ((0, 16), (1, 2)))
    key_rows = centred(key_list[1], (TOKENS, HD), 1.0, 6.0, ((0, 16), (1, 2)))
    value_rows = draw_value_rows(jax.random.fold_in(key_list[5], 71), 0)
    gate_rows = centred(key_list[3], (TOKENS, HD), 2.0, 8.0, ((0, 16), (1, 2)))
    cotangent = centred(key_list[4], (TOKENS, HD), 1.0, 6.0, ((0, 16), (1, 2)))
    return {"queries": queries, "key_rows": key_rows, "value_rows": value_rows, "gate_rows": gate_rows, "cotangent": cotangent}


EPSILON = 1e-06
HIGH = lax.Precision.HIGHEST

def silu_slope(x):
    sig = jax.nn.sigmoid(x)
    return sig * (1.0 + x * (1.0 - sig))

def low_round(x):
    return lax.optimization_barrier(x.astype(jnp.bfloat16)).astype(jnp.float32)

def reference(queries, key_rows, value_rows, gate_rows, cotangent):
    width = H * DH
    q_float = queries.astype(jnp.float32)
    k_float = key_rows.astype(jnp.float32)
    lifted_q = jax.nn.silu(q_float).astype(jnp.bfloat16)
    lifted_k = jax.nn.silu(k_float).astype(jnp.bfloat16)

    def split(x):
        return x.astype(jnp.float32).reshape(N_CTX, TOK_DEV, H, DH)
    blocks_q = split(lifted_q)
    blocks_k = split(lifted_k)
    blocks_v = split(value_rows)
    causal = (lax.broadcasted_iota(jnp.int32, (TOK_DEV, TOK_DEV), 0) >= lax.broadcasted_iota(jnp.int32, (TOK_DEV, TOK_DEV), 1)).astype(jnp.float32)

    def forward(state, block):
        bq, bk, bv = block
        scores = jnp.einsum('thd,shd->hts', bq, bk, precision=HIGH) * causal[None]
        weights = low_round(scores)
        state_low = low_round(state)
        out = jnp.einsum('hts,shd->thd', weights, bv, precision=HIGH) + jnp.einsum('thd,hde->the', bq, state_low, precision=HIGH)
        local = jnp.einsum('thd,the->hde', bk, bv, precision=HIGH)
        return (state + local, (out, state))
    zero_state = jnp.zeros((H, DH, DH), jnp.float32)
    final, (outs, states) = lax.scan(forward, zero_state, (blocks_q, blocks_k, blocks_v))
    attended = outs.reshape(TOKENS, width)
    sumsq = lax.optimization_barrier(jnp.sum(attended * attended, axis=1, keepdims=True))
    rms = jnp.sqrt(sumsq / width + EPSILON)
    normed = attended / rms
    sig = jax.nn.sigmoid(gate_rows.astype(jnp.float32))
    grad_out = cotangent.astype(jnp.float32)
    grad_gates = (grad_out * normed * sig * (1.0 - sig)).astype(jnp.bfloat16)
    gated = grad_out * sig
    inner = lax.optimization_barrier(jnp.sum(gated * normed, axis=1, keepdims=True))
    d_attn = ((gated - normed * inner / width) / rms).astype(jnp.bfloat16)
    blocks_d = split(d_attn)

    def backward(carry, block):
        bq, bk, bv, bd, state = block
        scores = jnp.einsum('thd,shd->hts', bq, bk, precision=HIGH) * causal[None]
        weights = low_round(scores)
        d_scores = jnp.einsum('the,she->hts', bd, bv, precision=HIGH) * causal[None]
        d_weights = low_round(d_scores)
        state_low = low_round(state)
        carry_low = low_round(carry)
        grad_lq = jnp.einsum('hts,shd->thd', d_weights, bk, precision=HIGH) + jnp.einsum('the,hde->thd', bd, state_low, precision=HIGH)
        grad_lk = jnp.einsum('hts,thd->shd', d_weights, bq, precision=HIGH) + jnp.einsum('she,hde->shd', bv, carry_low, precision=HIGH)
        grad_v = jnp.einsum('hts,the->she', weights, bd, precision=HIGH) + jnp.einsum('shd,hde->she', bk, carry_low, precision=HIGH)
        local = jnp.einsum('thd,the->hde', bq, bd, precision=HIGH)
        return (carry + local, (grad_lq, grad_lk, grad_v))
    last, (gq, gk, gv) = lax.scan(backward, zero_state, (blocks_q, blocks_k, blocks_v, blocks_d, states), reverse=True)
    grad_queries = (gq.reshape(TOKENS, width) * silu_slope(q_float)).astype(jnp.bfloat16)
    grad_keys = (gk.reshape(TOKENS, width) * silu_slope(k_float)).astype(jnp.bfloat16)
    grad_values = gv.reshape(TOKENS, width).astype(jnp.bfloat16)
    return (grad_queries, grad_keys, grad_values, grad_gates)
```

```python
import functools

import jax
import jax.numpy as jnp
from jax import lax
from jax.experimental import pallas as pl
from jax.experimental.pallas import tpu as pltpu
from jax.sharding import PartitionSpec as P

H = 32
DH = 128
EPSILON = 1e-06
QUAD = 4
F32 = jnp.float32
BF16 = jnp.bfloat16
EXACT = lax.Precision.HIGHEST


def dot(a, b, ca, cb, precision=None):
    return lax.dot_general(
        a, b, (((ca,), (cb,)), ((), ())), precision=precision, preferred_element_type=F32
    )


def sigmoid(x):
    return 0.5 + 0.5 * jnp.tanh(0.5 * x)


def core_of():
    return lax.rem(lax.axis_index("ctx"), 2)


def chip_of():
    return lax.rem(lax.axis_index("ctx") // 2, QUAD)


def params():
    return pltpu.CompilerParams(vmem_limit_bytes=48 * 1024 * 1024)


class Plan:
    def __init__(self, rows, width):
        self.rows, self.width = rows, width
        self.heads = width // DH
        self.half = self.heads // 2
        self.group = 4 if self.half % 4 == 0 else self.half
        self.per_half = self.half // self.group
        self.steps = 2 * self.per_half
        self.state = self.half * DH
        self.part = self.state // QUAD

    def place(self, step):
        side = lax.rem(step // self.per_half + 1 + core_of(), 2)
        return side * self.per_half + lax.rem(step, self.per_half)

    def given(self):
        return pl.BlockSpec((self.rows, self.group * DH), lambda i: (0, self.place(i)))

    def kept(self):
        return pl.BlockSpec((self.rows, self.group * DH), lambda i: (0, i))

    def square(self):
        return pl.BlockSpec((self.group, self.rows, self.rows), lambda i: (i, 0, 0))

    def whole(self, *shape):
        return pl.BlockSpec(shape, lambda i: (0,) * len(shape))

    def low(self):
        return jax.ShapeDtypeStruct((self.rows, self.width), BF16)

    def full(self):
        return jax.ShapeDtypeStruct((self.rows, self.width), F32)

    def halves_spec(self):
        block = (self.group * DH, DH)
        last = self.per_half - 1
        return [
            pl.BlockSpec(block, lambda i: (jnp.minimum(i, last), 0)),
            pl.BlockSpec(block, lambda i: (jnp.maximum(i - last - 1, 0), 0)),
        ]

    def halves(self):
        return [jax.ShapeDtypeStruct((self.state, DH), F32)] * 2


def store_half(plan, send_ref, keep_ref, g, value):
    step = pl.program_id(0)

    @pl.when(step < plan.per_half)
    def _():
        send_ref[g * DH : (g + 1) * DH, :] = value

    @pl.when(step >= plan.per_half)
    def _():
        keep_ref[g * DH : (g + 1) * DH, :] = value


def head(g):
    return slice(g * DH, (g + 1) * DH)


def key_state_kernel(plan, k_ref, v_ref, send_ref, keep_ref):
    for g in range(plan.group):
        x = k_ref[:, head(g)].astype(F32)
        lifted = (x * sigmoid(x)).astype(BF16)
        store_half(plan, send_ref, keep_ref, g, dot(lifted, v_ref[:, head(g)], 0, 0))


def causal_mask(rows):
    return lax.broadcasted_iota(jnp.int32, (rows, rows), 0) >= lax.broadcasted_iota(
        jnp.int32, (rows, rows), 1
    )


def local_kernel(plan, q_ref, k_ref, v_ref, gate_ref, cot_ref, lq_ref, w_ref, att_ref, gated_ref):
    causal = causal_mask(plan.rows)
    for g in range(plan.group):
        q = q_ref[:, head(g)].astype(F32)
        k = k_ref[:, head(g)].astype(F32)
        lq = (q * sigmoid(q)).astype(BF16)
        lk = (k * sigmoid(k)).astype(BF16)
        lq_ref[:, head(g)] = lq
        weights = jnp.where(causal, dot(lq, lk, 1, 1), 0.0).astype(BF16)
        w_ref[g] = weights
        att_ref[:, head(g)] = dot(weights, v_ref[:, head(g)], 1, 0)
        gated_ref[:, head(g)] = cot_ref[:, head(g)].astype(F32) * sigmoid(
            gate_ref[:, head(g)].astype(F32)
        )


def place_state(plan, reverse, own, far, near_add, far_add, state_ref):
    add = core_of() == (0 if reverse else 1)
    chip = chip_of()
    for k in range(QUAD):
        at = pl.multiple_of((chip ^ k) * plan.part, plan.part)
        here = pl.ds(at, plan.part)
        state_ref[pl.ds(pl.multiple_of(plan.state + at, plan.part), plan.part), :] = (
            own[k][...] + jnp.where(add, near_add[here, :], 0.0)
        ).astype(BF16)
        state_ref[here, :] = (far[k][...] + jnp.where(add, far_add[here, :], 0.0)).astype(BF16)


def attend_kernel(plan, *refs):
    own, far, (near_add, far_add) = refs[:4], refs[4:8], refs[8:10]
    lq_ref, local_ref, gated_ref, state_ref, att_ref, sums_ref, square, inner = refs[10:]
    step = pl.program_id(0)

    @pl.when(step == 0)
    def _():
        place_state(plan, False, own, far, near_add, far_add, state_ref)
        square[...] = jnp.zeros_like(square)
        inner[...] = jnp.zeros_like(inner)

    for g in range(plan.group):
        at = pl.multiple_of((step * plan.group + g) * DH, DH)
        att = local_ref[:, head(g)] + dot(lq_ref[:, head(g)], state_ref[pl.ds(at, DH), :], 1, 0)
        att_ref[:, head(g)] = att
        square[...] += att * att
        inner[...] += gated_ref[:, head(g)] * att

    @pl.when(step == plan.steps - 1)
    def _():
        line = lax.broadcasted_iota(jnp.int32, (8, DH), 0)
        sums_ref[...] = dot(
            jnp.where(line == 0, 1.0, 0.0), square[...], 1, 1, EXACT
        ) + dot(jnp.where(line == 1, 1.0, 0.0), inner[...], 1, 1, EXACT)


def grad_kernel(plan, mine_ref, theirs_ref, att_ref, gated_ref, lq_ref, d_ref, send_ref, keep_ref, inv_ref, coef):
    step = pl.program_id(0)

    @pl.when(step == 0)
    def _():
        total = mine_ref[...] + theirs_ref[...]
        line = lax.broadcasted_iota(jnp.int32, (8, DH), 0)
        sumsq = dot(total, jnp.where(line == 0, 1.0, 0.0), 0, 0, EXACT)
        raw = dot(total, jnp.where(line == 1, 1.0, 0.0), 0, 0, EXACT)
        inv = 1.0 / jnp.sqrt(sumsq * (1.0 / (H * DH)) + EPSILON)
        inv_ref[...] = inv
        coef[...] = raw * inv * (1.0 / (H * DH)) * inv * inv

    for g in range(plan.group):
        d = (gated_ref[:, head(g)] * inv_ref[...] - att_ref[:, head(g)] * coef[...]).astype(BF16)
        d_ref[:, head(g)] = d
        store_half(plan, send_ref, keep_ref, g, dot(lq_ref[:, head(g)], d, 0, 0))


def inside_kernel(plan, state_ref, inv_ref, w_ref, d_ref, lq_ref, att_ref, gated_ref, q_ref, k_ref, v_ref, gate_ref, gq_ref, gg_ref, pk_ref, pv_ref):
    step = pl.program_id(0)
    causal = causal_mask(plan.rows)
    for g in range(plan.group):
        at = pl.multiple_of((step * plan.group + g) * DH, DH)
        d = d_ref[:, head(g)]
        k = k_ref[:, head(g)].astype(F32)
        lk = (k * sigmoid(k)).astype(BF16)
        dw = jnp.where(causal, dot(d, v_ref[:, head(g)], 1, 1), 0.0).astype(BF16)
        glq = dot(dw, lk, 1, 0) + dot(d, state_ref[pl.ds(at, DH), :], 1, 1)
        q = q_ref[:, head(g)].astype(F32)
        sig = sigmoid(q)
        gq_ref[:, head(g)] = (glq * (sig * (1.0 + q * (1.0 - sig)))).astype(BF16)
        pk_ref[:, head(g)] = dot(dw, lq_ref[:, head(g)], 0, 0)
        pv_ref[:, head(g)] = dot(w_ref[g], d, 0, 0)
        gate = sigmoid(gate_ref[:, head(g)].astype(F32))
        gg_ref[:, head(g)] = (
            gated_ref[:, head(g)] * (att_ref[:, head(g)] * inv_ref[...]) * (1.0 - gate)
        ).astype(BF16)


def finish_kernel(plan, *refs):
    own, far, (near_add, far_add) = refs[:4], refs[4:8], refs[8:10]
    k_ref, v_ref, pk_ref, pv_ref, gk_ref, gv_ref, state_ref = refs[10:]
    step = pl.program_id(0)

    @pl.when(step == 0)
    def _():
        place_state(plan, True, own, far, near_add, far_add, state_ref)

    for g in range(plan.group):
        at = pl.multiple_of((step * plan.group + g) * DH, DH)
        state = state_ref[pl.ds(at, DH), :]
        k = k_ref[:, head(g)].astype(F32)
        sig = sigmoid(k)
        lk = (k * sig).astype(BF16)
        gv_ref[:, head(g)] = (pv_ref[:, head(g)] + dot(lk, state, 1, 0)).astype(BF16)
        glk = pk_ref[:, head(g)] + dot(v_ref[:, head(g)], state, 1, 1)
        gk_ref[:, head(g)] = (glk * (sig * (1.0 + k * (1.0 - sig)))).astype(BF16)


def split_kernel(plan, keep_ref, got_ref, *outs):
    chip = chip_of()
    for k in range(QUAD):
        here = pl.ds(pl.multiple_of((chip ^ k) * plan.part, plan.part), plan.part)
        outs[k][...] = keep_ref[here, :] + got_ref[here, :]


def before_kernel(reverse, span, *refs):
    parts, got_ref, base, outs = refs[:4], refs[4], refs[5:-4], refs[-4:]
    chip = chip_of()
    far = lax.rem(lax.axis_index("ctx") // span, 2) == (0 if reverse else 1)
    start = jnp.where(far, got_ref[...], 0.0)
    for more in base:
        start = start + more[...]
    for k in range(QUAD):
        total = start
        for m in range(QUAD):
            first = (chip ^ m) > (chip ^ k) if reverse else (chip ^ m) < (chip ^ k)
            total = total + jnp.where(first, parts[m][...], 0.0)
        outs[k][...] = total


def swap(x, distance):
    count = lax.axis_size("ctx")
    return lax.ppermute(x, "ctx", [(i, i ^ distance) for i in range(count)])


def carried_in(plan, send, keep, reverse):
    count = lax.axis_size("ctx")
    near_add = swap(send, 1)
    far_add = swap(keep, 1)
    piece = jax.ShapeDtypeStruct((plan.part, DH), F32)
    mine = pl.pallas_call(
        functools.partial(split_kernel, plan), out_shape=[piece] * QUAD, compiler_params=params()
    )(keep, near_add)
    parts = [mine[0]] + [swap(mine[k], 2 * k) for k in range(1, QUAD)]
    total = (parts[0] + parts[1]) + (parts[2] + parts[3])
    base = []
    span = 2 * QUAD
    while True:
        got = swap(total, span)
        if 2 * span >= count:
            break
        far = lax.rem(lax.axis_index("ctx") // span, 2) == (0 if reverse else 1)
        term = jnp.where(far, got, 0.0)
        base = [base[0] + term] if base else [term]
        total = total + got
        span *= 2
    outs = pl.pallas_call(
        functools.partial(before_kernel, reverse, span),
        out_shape=[piece] * QUAD,
        compiler_params=params(),
    )(*parts, got, *base)
    own = [outs[0]] + [swap(outs[k], 2 * k) for k in range(1, QUAD)]
    far = [swap(x, 1) for x in own]
    return own + far + [near_add, far_add]


def head_total(sums):
    count = lax.axis_size("head")
    if count == 2:
        return sums, lax.ppermute(sums, "head", [(0, 1), (1, 0)])
    return lax.psum(sums, "head"), jnp.zeros_like(sums)


def per_device(queries, key_rows, value_rows, gate_rows, cotangent):
    rows, width = queries.shape
    plan = Plan(rows, width)
    given, kept = plan.given(), plan.kept()
    pieces = [plan.whole(plan.part, DH)] * 8 + [plan.whole(plan.state, DH)] * 2
    state_spec = plan.whole(2 * plan.state, DH)
    state_shape = jax.ShapeDtypeStruct((2 * plan.state, DH), BF16)
    sums_spec = plan.whole(8, rows)
    wide_spec = plan.whole(rows, DH)

    def call(kernel, in_specs, out_specs, out_shape, scratch=()):
        return pl.pallas_call(
            functools.partial(kernel, plan),
            grid=(plan.steps,),
            in_specs=in_specs,
            out_specs=out_specs,
            out_shape=out_shape,
            scratch_shapes=list(scratch),
            compiler_params=params(),
        )

    send, keep = call(key_state_kernel, [given] * 2, plan.halves_spec(), plan.halves())(
        key_rows, value_rows
    )
    lq, weights, local, gated = call(
        local_kernel,
        [given] * 5,
        [kept, plan.square(), kept, kept],
        [
            plan.low(),
            jax.ShapeDtypeStruct((plan.heads, rows, rows), BF16),
            plan.full(),
            plan.full(),
        ],
    )(queries, key_rows, value_rows, gate_rows, cotangent)
    arrived = carried_in(plan, send, keep, False)
    state, attended, sums = call(
        attend_kernel,
        pieces + [kept] * 3,
        [state_spec, kept, sums_spec],
        [state_shape, plan.full(), jax.ShapeDtypeStruct((8, rows), F32)],
        [pltpu.VMEM((rows, DH), F32)] * 2,
    )(*arrived, lq, local, gated)
    mine, theirs = head_total(sums)
    d_attn, send, keep, inverse = call(
        grad_kernel,
        [sums_spec] * 2 + [kept] * 3,
        [kept] + plan.halves_spec() + [wide_spec],
        [plan.low()] + plan.halves() + [jax.ShapeDtypeStruct((rows, DH), F32)],
        [pltpu.VMEM((rows, DH), F32)],
    )(mine, theirs, attended, gated, lq)
    grad_queries, grad_gates, part_k, part_v = call(
        inside_kernel,
        [state_spec, wide_spec, plan.square()] + [kept] * 4 + [given] * 4,
        [given] * 2 + [kept] * 2,
        [plan.low()] * 2 + [plan.full()] * 2,
    )(
        state, inverse, weights, d_attn, lq, attended, gated,
        queries, key_rows, value_rows, gate_rows,
    )
    arrived = carried_in(plan, send, keep, True)
    grad_keys, grad_values = call(
        finish_kernel,
        pieces + [given] * 2 + [kept] * 2,
        [given] * 2,
        [plan.low()] * 2,
        [pltpu.VMEM((2 * plan.state, DH), BF16)],
    )(*arrived, key_rows, value_rows, part_k, part_v)
    return (grad_queries, grad_keys, grad_values, grad_gates)


def solution(mesh):
    spec = P("ctx", "head")
    return jax.shard_map(
        per_device, mesh=mesh, in_specs=(spec,) * 5, out_specs=(spec,) * 4, check_vma=False
    )
```

```python
import functools

import jax
import jax.numpy as jnp
from jax import lax
from jax.experimental import pallas as pl
from jax.experimental.pallas import tpu as pltpu
from jax.sharding import PartitionSpec as P

H = 32
DH = 128
EPSILON = 1e-06
QUAD = 4
CHUNKS = 1
F32 = jnp.float32
BF16 = jnp.bfloat16
EXACT = lax.Precision.HIGHEST
SMALL = 16 * 1024 * 1024
LARGE = 60 * 1024 * 1024
ANY = pl.BlockSpec(memory_space=pl.ANY)
VMEM = pl.BlockSpec(memory_space=pltpu.VMEM)


def dot(a, b, ca, cb, precision=None):
    return lax.dot_general(
        a, b, (((ca,), (cb,)), ((), ())), precision=precision, preferred_element_type=F32
    )


def sigmoid(x):
    return 0.5 + 0.5 * jnp.tanh(0.5 * x)


def core_of():
    return lax.rem(lax.axis_index("ctx"), 2)


def chip_of():
    return lax.rem(lax.axis_index("ctx") // 2, QUAD)


def head(g):
    return slice(g * DH, (g + 1) * DH)


def after(values, done):
    flat, tree = jax.tree.flatten(values)
    out = lax.optimization_barrier(tuple(flat) + tuple(jax.tree.leaves(done)))
    return jax.tree.unflatten(tree, out[: len(flat)])


class Plan:
    def __init__(self, rows, width):
        self.rows, self.width = rows, width
        self.heads = width // DH
        self.group = self.heads // (2 * CHUNKS)
        self.span = self.group * DH
        self.part = self.span // QUAD
        self.tall = jax.ShapeDtypeStruct((self.span, DH), F32)
        self.piece = jax.ShapeDtypeStruct((self.part, DH), F32)
        self.low = jax.ShapeDtypeStruct((rows, self.span), BF16)
        self.full = jax.ShapeDtypeStruct((rows, self.span), F32)
        self.wide = jax.ShapeDtypeStruct((rows, DH), F32)
        self.square = jax.ShapeDtypeStruct((self.group, rows, rows), BF16)
        self.state = jax.ShapeDtypeStruct((self.span, DH), BF16)
        self.given = jax.ShapeDtypeStruct((rows, width), BF16)
        self.sums = jax.ShapeDtypeStruct((8, rows), F32)

    def start(self, chunk, side):
        half = lax.rem(core_of() + 1 + side, 2)
        return pl.multiple_of((half * CHUNKS + chunk) * self.span, self.span)

    def columns(self, chunk, side, g=None):
        start = self.start(chunk, side)
        if g is None:
            return pl.ds(start, self.span)
        return pl.ds(pl.multiple_of(start + g * DH, DH), DH)


def run(kernel, out_shape, *args, scratch=(), in_specs=None, out_specs=None, limit=SMALL, aliases=None):
    extra = {}
    if in_specs is not None:
        extra["in_specs"] = in_specs
    if out_specs is not None:
        extra["out_specs"] = out_specs
    if aliases:
        extra["input_output_aliases"] = aliases
    return pl.pallas_call(
        kernel,
        out_shape=out_shape,
        scratch_shapes=list(scratch),
        compiler_params=pltpu.CompilerParams(vmem_limit_bytes=limit),
        **extra,
    )(*args)


def key_state(k, v):
    return dot((k * sigmoid(k)).astype(BF16), v, 0, 0)


def first_kernel(plan, order, k_hbm, v_hbm, k_ref, v_ref, out_ref, sems):
    copies = []
    for n, where in enumerate(order):
        at = (slice(None), plan.columns(*where))
        for m, (source, target) in enumerate(((k_hbm, k_ref), (v_hbm, v_ref))):
            copy = pltpu.make_async_copy(source.at[at], target.at[at], sems.at[2 * n + m])
            copy.start()
            copies.append(copy)
    copies[0].wait()
    copies[1].wait()
    for g in range(plan.group):
        at = plan.columns(*order[0], g)
        out_ref[head(g), :] = key_state(k_ref[:, at].astype(F32), v_ref[:, at])
    for copy in copies[2:]:
        copy.wait()


def next_kernel(plan, where, k_ref, v_ref, out_ref):
    for g in range(plan.group):
        at = plan.columns(*where, g)
        out_ref[head(g), :] = key_state(k_ref[:, at].astype(F32), v_ref[:, at])


def causal_mask(rows):
    return lax.broadcasted_iota(jnp.int32, (rows, rows), 0) >= lax.broadcasted_iota(
        jnp.int32, (rows, rows), 1
    )


def local_kernel(plan, where, q_ref, k_ref, v_ref, gate_ref, cot_ref, lq_ref, lk_ref, w_ref, att_ref, gated_ref):
    causal = causal_mask(plan.rows)
    for g in range(plan.group):
        at = plan.columns(*where, g)
        q = q_ref[:, at].astype(F32)
        k = k_ref[:, at].astype(F32)
        lq = (q * sigmoid(q)).astype(BF16)
        lk = (k * sigmoid(k)).astype(BF16)
        lq_ref[:, head(g)] = lq
        lk_ref[:, head(g)] = lk
        weights = jnp.where(causal, dot(lq, lk, 1, 1), 0.0).astype(BF16)
        w_ref[g] = weights
        att_ref[:, head(g)] = dot(weights, v_ref[:, at], 1, 0)
        gated_ref[:, head(g)] = cot_ref[:, at].astype(F32) * sigmoid(gate_ref[:, at].astype(F32))


def place_state(plan, reverse, pieces, add_ref, state_ref):
    add = core_of() == (0 if reverse else 1)
    chip = chip_of()
    for k in range(QUAD):
        here = pl.ds(pl.multiple_of((chip ^ k) * plan.part, plan.part), plan.part)
        state_ref[here, :] = (pieces[k][...] + jnp.where(add, add_ref[here, :], 0.0)).astype(BF16)


def attend_kernel(plan, first, last, *refs):
    pieces, add_ref = refs[:4], refs[4]
    lq_ref, local_ref, gated_ref = refs[5:8]
    refs = refs[8:]
    if not first:
        square, inner = refs[0][...], refs[1][...]
        refs = refs[2:]
    state_ref, att_ref = refs[:2]
    place_state(plan, False, pieces, add_ref, state_ref)
    for g in range(plan.group):
        att = local_ref[:, head(g)] + dot(lq_ref[:, head(g)], state_ref[head(g), :], 1, 0)
        att_ref[:, head(g)] = att
        if first and g == 0:
            square, inner = att * att, gated_ref[:, head(g)] * att
        else:
            square, inner = square + att * att, inner + gated_ref[:, head(g)] * att
    if last:
        line = lax.broadcasted_iota(jnp.int32, (8, DH), 0)
        refs[2][...] = dot(jnp.where(line == 0, 1.0, 0.0), square, 1, 1, EXACT) + dot(
            jnp.where(line == 1, 1.0, 0.0), inner, 1, 1, EXACT
        )
    else:
        refs[2][...] = square
        refs[3][...] = inner


def grad_kernel(plan, first, a_ref, b_ref, att_ref, gated_ref, lq_ref, d_ref, sum_ref, *more):
    if first:
        total = a_ref[...] + b_ref[...]
        line = lax.broadcasted_iota(jnp.int32, (8, DH), 0)
        sumsq = dot(total, jnp.where(line == 0, 1.0, 0.0), 0, 0, EXACT)
        raw = dot(total, jnp.where(line == 1, 1.0, 0.0), 0, 0, EXACT)
        inv = 1.0 / jnp.sqrt(sumsq * (1.0 / (H * DH)) + EPSILON)
        coef = raw * inv * (1.0 / (H * DH)) * inv * inv
        more[0][...] = inv
        more[1][...] = coef
    else:
        inv, coef = a_ref[...], b_ref[...]
    for g in range(plan.group):
        d = (gated_ref[:, head(g)] * inv - att_ref[:, head(g)] * coef).astype(BF16)
        d_ref[:, head(g)] = d
        sum_ref[head(g), :] = dot(lq_ref[:, head(g)], d, 0, 0)


def inside_kernel(plan, where, first, *refs):
    (state_ref, inv_ref, w_ref, d_ref, lq_ref, lk_ref, att_ref, gated_ref) = refs[:8]
    q_ref, v_ref, gate_ref = refs[8:11]
    gq_hbm, gg_hbm, pk_ref, pv_ref, gq, gg, sems = refs[11 if first else 13 :]
    causal = causal_mask(plan.rows)
    for g in range(plan.group):
        at = plan.columns(*where, g)
        d = d_ref[:, head(g)]
        dw = jnp.where(causal, dot(d, v_ref[:, at], 1, 1), 0.0).astype(BF16)
        glq = dot(dw, lk_ref[:, head(g)], 1, 0) + dot(d, state_ref[head(g), :], 1, 1)
        q = q_ref[:, at].astype(F32)
        sig = sigmoid(q)
        gq[:, head(g)] = (glq * (sig * (1.0 + q * (1.0 - sig)))).astype(BF16)
        pk_ref[:, head(g)] = dot(dw, lq_ref[:, head(g)], 0, 0)
        pv_ref[:, head(g)] = dot(w_ref[g], d, 0, 0)
        gate = sigmoid(gate_ref[:, at].astype(F32))
        gg[:, head(g)] = (
            gated_ref[:, head(g)] * (att_ref[:, head(g)] * inv_ref[...]) * (1.0 - gate)
        ).astype(BF16)
    send_out(plan, where, ((gq, gq_hbm), (gg, gg_hbm)), sems)


def send_out(plan, where, pairs, sems):
    at = (slice(None), plan.columns(*where))
    copies = [
        pltpu.make_async_copy(source, target.at[at], sems.at[n])
        for n, (source, target) in enumerate(pairs)
    ]
    for copy in copies:
        copy.start()
    for copy in copies:
        copy.wait()


def finish_kernel(plan, where, first, *refs):
    pieces, add_ref = refs[:4], refs[4]
    k_ref, v_ref, lk_ref, pk_ref, pv_ref = refs[5:10]
    gk_hbm, gv_hbm, state_ref, gk, gv, sems = refs[10 if first else 12 :]
    place_state(plan, True, pieces, add_ref, state_ref)
    for g in range(plan.group):
        at = plan.columns(*where, g)
        state = state_ref[head(g), :]
        k = k_ref[:, at].astype(F32)
        sig = sigmoid(k)
        gv[:, head(g)] = (pv_ref[:, head(g)] + dot(lk_ref[:, head(g)], state, 1, 0)).astype(BF16)
        glk = pk_ref[:, head(g)] + dot(v_ref[:, at], state, 1, 1)
        gk[:, head(g)] = (glk * (sig * (1.0 + k * (1.0 - sig)))).astype(BF16)
    send_out(plan, where, ((gk, gk_hbm), (gv, gv_hbm)), sems)


def split_kernel(plan, keep_ref, got_ref, *outs):
    chip = chip_of()
    for k in range(QUAD):
        here = pl.ds(pl.multiple_of((chip ^ k) * plan.part, plan.part), plan.part)
        outs[k][...] = keep_ref[here, :] + got_ref[here, :]


def before_kernel(reverse, span, *refs):
    parts, got_ref, base, outs = refs[:4], refs[4], refs[5:-4], refs[-4:]
    chip = chip_of()
    far = lax.rem(lax.axis_index("ctx") // span, 2) == (0 if reverse else 1)
    start = jnp.where(far, got_ref[...], 0.0)
    for more in base:
        start = start + more[...]
    for k in range(QUAD):
        total = start
        for m in range(QUAD):
            first = (chip ^ m) > (chip ^ k) if reverse else (chip ^ m) < (chip ^ k)
            total = total + jnp.where(first, parts[m][...], 0.0)
        outs[k][...] = total


def swap(x, distance):
    count = lax.axis_size("ctx")
    return lax.ppermute(x, "ctx", [(i, i ^ distance) for i in range(count)])


def gather_sums(plan, keep, near):
    mine = run(functools.partial(split_kernel, plan), [plan.piece] * QUAD, keep, near)
    return [mine[0]] + [swap(mine[k], 2 * k) for k in range(1, QUAD)]


def across(parts, reverse):
    count = lax.axis_size("ctx")
    total = (parts[0] + parts[1]) + (parts[2] + parts[3])
    base = []
    span = 2 * QUAD
    while True:
        got = swap(total, span)
        if 2 * span >= count:
            return got, base, span
        far = lax.rem(lax.axis_index("ctx") // span, 2) == (0 if reverse else 1)
        term = jnp.where(far, got, 0.0)
        base = [base[0] + term] if base else [term]
        total = total + got
        span *= 2


def hand_out(plan, parts, got, base, span, reverse):
    outs = run(
        functools.partial(before_kernel, reverse, span),
        [plan.piece] * QUAD,
        *parts,
        got,
        *base,
    )
    return [outs[0]] + [swap(outs[k], 2 * k) for k in range(1, QUAD)]


def head_total(sums):
    if lax.axis_size("head") == 2:
        return sums, lax.ppermute(sums, "head", [(0, 1), (1, 0)])
    return lax.psum(sums, "head"), jnp.zeros_like(sums)


def carried(plan, sums_of, work, reverse):
    chunks = range(CHUNKS)
    near = [swap(sums_of[c, 0], 1) for c in chunks]
    parts = [gather_sums(plan, sums_of[c, 1], near[c]) for c in chunks]
    far_add = [swap(after(sums_of[c, 1], near[c]), 1) for c in chunks]
    results = []
    held = parts[-1][0]
    done = [t(held) for t in work[0]]
    results += done
    parts = [after(p, done) for p in parts]
    crossed = [across(p, reverse) for p in parts]
    done = [t(parts[-1][0]) for t in work[1]]
    results += done
    crossed = [(after(got, done), base, span) for got, base, span in crossed]
    pieces = {}
    for c in chunks:
        own = hand_out(plan, parts[c], *crossed[c], reverse)
        pieces[c, 1] = own + [near[c]]
        pieces[c, 0] = [swap(x, 1) for x in own] + [far_add[c]]
    return pieces, results


def per_device(queries, key_rows, value_rows, gate_rows, cotangent):
    plan = Plan(*queries.shape)
    groups = [(c, side) for c in range(CHUNKS) for side in (0, 1)]
    late = [(c, side) for c in range(CHUNKS) for side in (1, 0)]
    count = len(groups)
    k, v, first_sum = run(
        functools.partial(first_kernel, plan, groups),
        [plan.given, plan.given, plan.tall],
        key_rows,
        value_rows,
        scratch=[pltpu.SemaphoreType.DMA((2 * count,))],
        in_specs=[ANY, ANY],
        limit=LARGE,
    )
    sums = {groups[0]: first_sum}
    for where in groups[1:]:
        sums[where] = run(functools.partial(next_kernel, plan, where), plan.tall, k, v)

    def local(where):
        def thunk(held):
            args = after((queries, k, v, gate_rows, cotangent), held)
            return run(
                functools.partial(local_kernel, plan, where),
                [plan.low, plan.low, plan.square, plan.full, plan.full],
                *args,
            )

        return thunk

    thunks = [local(where) for where in groups]
    pieces, made = carried(plan, sums, (thunks[: count // 2], thunks[count // 2 :]), False)
    made = dict(zip(groups, made))
    lq, lk, weights, inside, gated = ({w: made[w][n] for w in groups} for n in range(5))
    state, attended, running = {}, {}, ()
    for n, where in enumerate(late):
        last = n == count - 1
        state[where], attended[where], *running = run(
            functools.partial(attend_kernel, plan, n == 0, last),
            [plan.state, plan.full] + ([plan.sums] if last else [plan.wide] * 2),
            *pieces[where],
            lq[where],
            inside[where],
            gated[where],
            *running,
        )
    scales = head_total(running[0])
    d_attn, sums = {}, {}
    for n, where in enumerate(groups):
        d_attn[where], sums[where], *more = run(
            functools.partial(grad_kernel, plan, n == 0),
            [plan.low, plan.tall] + ([plan.wide] * 2 if n == 0 else []),
            *scales,
            attended[where],
            gated[where],
            lq[where],
        )
        scales = more or scales
    outer = []

    def inner(where):
        def thunk(held):
            first = not outer
            args = after(
                (
                    state[where], scales[0], weights[where], d_attn[where], lq[where], lk[where],
                    attended[where], gated[where], queries, v, gate_rows,
                ),
                held,
            )
            gq, gg, pk, pv = run(
                functools.partial(inside_kernel, plan, where, first),
                [plan.given, plan.given, plan.full, plan.full],
                *args,
                *outer,
                scratch=[pltpu.VMEM((plan.rows, plan.span), BF16)] * 2
                + [pltpu.SemaphoreType.DMA((2,))],
                in_specs=[VMEM] * 11 + [ANY] * len(outer),
                out_specs=[ANY, ANY, VMEM, VMEM],
                aliases={} if first else {11: 0, 12: 1},
            )
            outer[:] = [gq, gg]
            return pk, pv

        return thunk

    thunks = [inner(where) for where in groups]
    pieces, made = carried(plan, sums, (thunks[: count // 2], thunks[count // 2 :]), True)
    made = dict(zip(groups, made))
    ends = []
    for n, where in enumerate(late):
        ends = run(
            functools.partial(finish_kernel, plan, where, n == 0),
            [plan.given, plan.given],
            *pieces[where],
            k,
            v,
            lk[where],
            *made[where],
            *ends,
            scratch=[pltpu.VMEM((plan.span, DH), BF16)]
            + [pltpu.VMEM((plan.rows, plan.span), BF16)] * 2
            + [pltpu.SemaphoreType.DMA((2,))],
            in_specs=[VMEM] * 10 + [ANY] * len(ends),
            out_specs=[ANY, ANY],
            aliases={} if n == 0 else {10: 0, 11: 1},
        )
    return (outer[0], ends[0], ends[1], outer[1])


def solution(mesh):
    spec = P("ctx", "head")
    return jax.shard_map(
        per_device, mesh=mesh, in_specs=(spec,) * 5, out_specs=(spec,) * 4, check_vma=False
    )
```

```python
import functools

import jax
import jax.numpy as jnp
from jax import lax
from jax.experimental import pallas as pl
from jax.experimental.pallas import tpu as pltpu
from jax.sharding import PartitionSpec as P

H = 32
DH = 128
EPSILON = 1e-06
QUAD = 4
GATHER = ((0,1,2,3),(0,2,1,3))
HAND = ((0,1,2,3),(0,3,2,1))
CHUNKS = 1
BATCH = 4
F32 = jnp.float32
BF16 = jnp.bfloat16
SMALL = 16 * 1024 * 1024
LARGE = 60 * 1024 * 1024
ANY = pl.BlockSpec(memory_space=pl.ANY)
VMEM = pl.BlockSpec(memory_space=pltpu.VMEM)


def dot(a, b, ca, cb):
    return lax.dot_general(a, b, (((ca,), (cb,)), ((), ())), preferred_element_type=F32)


def sigmoid(x):
    return 0.5 + 0.5 * jnp.tanh(0.5 * x)


def thirds(x):
    first = x.astype(BF16)
    rest = x - first.astype(F32)
    second = rest.astype(BF16)
    return [first, second, (rest - second.astype(F32)).astype(BF16)]


def chooser(rows, width):
    line = lax.broadcasted_iota(jnp.int32, (rows, width), 0)
    column = lax.broadcasted_iota(jnp.int32, (rows, width), 1)
    return jnp.where(line == column // DH, 1.0, 0.0).astype(BF16)


def core_of():
    return lax.rem(lax.axis_index("ctx"), 2)


def chip_of():
    return lax.rem(lax.axis_index("ctx") // 2, QUAD)


def mate(orders, n, other=0):
    first, second = orders[0][n], orders[1][n]
    return first + (core_of() ^ other) * (second - first)


def head(g):
    return slice(g * DH, (g + 1) * DH)


def after(values, done):
    flat, tree = jax.tree.flatten(values)
    out = lax.optimization_barrier(tuple(flat) + tuple(jax.tree.leaves(done)))
    return jax.tree.unflatten(tree, out[: len(flat)])


class Plan:
    def __init__(self, rows, width):
        self.rows, self.width = rows, width
        self.heads = width // DH
        self.group = self.heads // (2 * CHUNKS)
        self.span = self.group * DH
        self.batch = BATCH if self.group % BATCH == 0 else 1
        self.part = self.span // QUAD
        self.tall = jax.ShapeDtypeStruct((self.span, DH), F32)
        self.piece = jax.ShapeDtypeStruct((self.part, DH), F32)
        self.low = jax.ShapeDtypeStruct((rows, self.span), BF16)
        self.full = jax.ShapeDtypeStruct((rows, self.span), F32)
        self.wide = jax.ShapeDtypeStruct((rows, DH), F32)
        self.square = jax.ShapeDtypeStruct((self.group, rows, rows), BF16)
        self.state = jax.ShapeDtypeStruct((self.span, DH), BF16)
        self.given = jax.ShapeDtypeStruct((rows, width), BF16)
        self.sums = jax.ShapeDtypeStruct((8, rows), F32)

    def start(self, chunk, side):
        half = lax.rem(core_of() + 1 + side, 2)
        return pl.multiple_of((half * CHUNKS + chunk) * self.span, self.span)

    def columns(self, chunk, side, g=None):
        start = self.start(chunk, side)
        if g is None:
            return pl.ds(start, self.span)
        return pl.ds(pl.multiple_of(start + g * DH, DH), DH)


def run(kernel, out_shape, *args, scratch=(), in_specs=None, out_specs=None, limit=SMALL, aliases=None):
    extra = {}
    if in_specs is not None:
        extra["in_specs"] = in_specs
    if out_specs is not None:
        extra["out_specs"] = out_specs
    if aliases:
        extra["input_output_aliases"] = aliases
    return pl.pallas_call(
        kernel,
        out_shape=out_shape,
        scratch_shapes=list(scratch),
        compiler_params=pltpu.CompilerParams(vmem_limit_bytes=limit),
        **extra,
    )(*args)


def key_state(k, v):
    return dot((k * sigmoid(k)).astype(BF16), v, 0, 0)


def first_kernel(plan, order, k_hbm, v_hbm, k_ref, v_ref, out_ref, sems):
    copies = []
    for n, where in enumerate(order):
        at = (slice(None), plan.columns(*where))
        for m, (source, target) in enumerate(((k_hbm, k_ref), (v_hbm, v_ref))):
            copy = pltpu.make_async_copy(source.at[at], target.at[at], sems.at[2 * n + m])
            copy.start()
            copies.append(copy)
    copies[0].wait()
    copies[1].wait()
    for g in range(plan.group):
        at = plan.columns(*order[0], g)
        out_ref[head(g), :] = key_state(k_ref[:, at].astype(F32), v_ref[:, at])
    for copy in copies[2:]:
        copy.wait()


def next_kernel(plan, where, k_ref, v_ref, out_ref):
    for g in range(plan.group):
        at = plan.columns(*where, g)
        out_ref[head(g), :] = key_state(k_ref[:, at].astype(F32), v_ref[:, at])


def causal_mask(rows):
    return lax.broadcasted_iota(jnp.int32, (rows, rows), 0) >= lax.broadcasted_iota(
        jnp.int32, (rows, rows), 1
    )


def local_kernel(plan, where, q_ref, k_ref, v_ref, gate_ref, cot_ref, lq_ref, lk_ref, w_ref, att_ref, gated_ref):
    causal = causal_mask(plan.rows)
    for g in range(plan.group):
        at = plan.columns(*where, g)
        q = q_ref[:, at].astype(F32)
        k = k_ref[:, at].astype(F32)
        lq = (q * sigmoid(q)).astype(BF16)
        lk = (k * sigmoid(k)).astype(BF16)
        lq_ref[:, head(g)] = lq
        lk_ref[:, head(g)] = lk
        weights = jnp.where(causal, dot(lq, lk, 1, 1), 0.0).astype(BF16)
        w_ref[g] = weights
        att_ref[:, head(g)] = dot(weights, v_ref[:, at], 1, 0)
        gated_ref[:, head(g)] = cot_ref[:, at].astype(F32) * sigmoid(gate_ref[:, at].astype(F32))


def place_state(plan, reverse, side, pieces, add_ref, state_ref):
    add = core_of() == (0 if reverse else 1)
    chip = chip_of()
    for k in range(QUAD):
        here = pl.ds(pl.multiple_of((chip ^ mate(HAND, k, 1 - side)) * plan.part, plan.part), plan.part)
        piece = pieces[k][...]
        for more in add_ref:
            piece = piece + jnp.where(add, more[here, :], 0.0)
        state_ref[here, :] = piece.astype(BF16)


def attend_kernel(plan, side, first, last, *refs):
    pieces, add_ref = refs[:4], refs[4 : 4 + side]
    refs = refs[4 + side :]
    lq_ref, local_ref, gated_ref = refs[:3]
    refs = refs[3:]
    if not first:
        square, inner = refs[0][...], refs[1][...]
        refs = refs[2:]
    state_ref, att_ref = refs[:2]
    place_state(plan, False, side, pieces, add_ref, state_ref)
    for g in range(plan.group):
        att = local_ref[:, head(g)] + dot(lq_ref[:, head(g)], state_ref[head(g), :], 1, 0)
        att_ref[:, head(g)] = att
        if first and g == 0:
            square, inner = att * att, gated_ref[:, head(g)] * att
        else:
            square, inner = square + att * att, inner + gated_ref[:, head(g)] * att
    if last:
        pick = chooser(8, 2 * DH)
        terms = thirds(jnp.concatenate([square, inner], axis=1))
        refs[2][...] = sum(dot(pick, term, 1, 1) for term in terms)
    else:
        refs[2][...] = square
        refs[3][...] = inner


def grad_kernel(plan, first, a_ref, b_ref, att_ref, gated_ref, lq_ref, d_ref, sum_ref, *more):
    if first:
        total = a_ref[...] + b_ref[...]
        sumsq, raw = total[0:1, :], total[1:2, :]
        inv = 1.0 / jnp.sqrt(sumsq * (1.0 / (H * DH)) + EPSILON)
        coef = raw * inv * (1.0 / (H * DH)) * inv * inv
        line = lax.broadcasted_iota(jnp.int32, total.shape, 0)
        rows = jnp.where(line == 0, inv, jnp.where(line == 1, coef, 0.0))
        pick = chooser(8, 2 * DH)
        both = sum(dot(term, pick, 0, 0) for term in thirds(rows))
        inv, coef = both[:, :DH], both[:, DH:]
        more[0][...] = inv
        more[1][...] = coef
    else:
        inv, coef = a_ref[...], b_ref[...]
    for g in range(plan.group):
        d = (gated_ref[:, head(g)] * inv - att_ref[:, head(g)] * coef).astype(BF16)
        d_ref[:, head(g)] = d
        sum_ref[head(g), :] = dot(lq_ref[:, head(g)], d, 0, 0)


def inside_kernel(plan, where, first, *refs):
    (state_ref, inv_ref, w_ref, d_ref, lq_ref, lk_ref, att_ref, gated_ref) = refs[:8]
    q_ref, v_ref, gate_ref = refs[8:11]
    gq_hbm, gg_hbm, pk_ref, pv_ref, gq, gg, sems = refs[11 if first else 13 :]
    causal = causal_mask(plan.rows)
    for g in range(plan.group):
        at = plan.columns(*where, g)
        d = d_ref[:, head(g)]
        dw = jnp.where(causal, dot(d, v_ref[:, at], 1, 1), 0.0).astype(BF16)
        glq = dot(dw, lk_ref[:, head(g)], 1, 0) + dot(d, state_ref[head(g), :], 1, 1)
        q = q_ref[:, at].astype(F32)
        sig = sigmoid(q)
        gq[:, head(g)] = (glq * (sig * (1.0 + q * (1.0 - sig)))).astype(BF16)
        pk_ref[:, head(g)] = dot(dw, lq_ref[:, head(g)], 0, 0)
        pv_ref[:, head(g)] = dot(w_ref[g], d, 0, 0)
        gate = sigmoid(gate_ref[:, at].astype(F32))
        gg[:, head(g)] = (
            gated_ref[:, head(g)] * (att_ref[:, head(g)] * inv_ref[...]) * (1.0 - gate)
        ).astype(BF16)
    send_out(plan, where, ((gq, gq_hbm), (gg, gg_hbm)), sems)


def send_out(plan, where, pairs, sems):
    at = (slice(None), plan.columns(*where))
    copies = [
        pltpu.make_async_copy(source, target.at[at], sems.at[n])
        for n, (source, target) in enumerate(pairs)
    ]
    for copy in copies:
        copy.start()
    for copy in copies:
        copy.wait()


def finish_kernel(plan, where, *refs):
    side = where[1]
    pieces, add_ref = refs[:4], refs[4 : 4 + side]
    refs = refs[4 + side :]
    k_ref, v_ref, lk_ref, pk_ref, pv_ref = refs[:5]
    if side:
        gk, gv, state_ref = refs[5:]
    else:
        gk_done, gv_done, gk_hbm, gv_hbm, state_ref, gk, gv, sems = refs[5:]
    copies = []

    def send(pairs, at):
        for source, target in pairs:
            copy = pltpu.make_async_copy(source, target.at[:, at], sems.at[len(copies)])
            copy.start()
            copies.append(copy)

    if not side:
        send(((gk_done, gk_hbm), (gv_done, gv_hbm)), plan.columns(where[0], 1))
    place_state(plan, True, side, pieces, add_ref, state_ref)
    for g in range(plan.group):
        at = plan.columns(*where, g)
        state = state_ref[head(g), :]
        k = k_ref[:, at].astype(F32)
        sig = sigmoid(k)
        gv[:, head(g)] = (pv_ref[:, head(g)] + dot(lk_ref[:, head(g)], state, 1, 0)).astype(BF16)
        glk = pk_ref[:, head(g)] + dot(v_ref[:, at], state, 1, 1)
        gk[:, head(g)] = (glk * (sig * (1.0 + k * (1.0 - sig)))).astype(BF16)
        if not side and (g + 1) % plan.batch == 0:
            first = g + 1 - plan.batch
            here = slice(first * DH, (g + 1) * DH)
            start = pl.multiple_of(plan.start(*where) + first * DH, DH)
            pairs = ((gk.at[:, here], gk_hbm), (gv.at[:, here], gv_hbm))
            send(pairs, pl.ds(start, plan.batch * DH))
    for copy in copies:
        copy.wait()


def split_kernel(plan, keep_ref, got_ref, *outs):
    chip = chip_of()
    for k in range(QUAD):
        here = pl.ds(pl.multiple_of((chip ^ mate(GATHER, k)) * plan.part, plan.part), plan.part)
        outs[k][...] = keep_ref[here, :] + got_ref[here, :]


def onward_kernel(plan, reverse, k, piece_ref, keep_ref, out_ref):
    here = pl.ds(pl.multiple_of((chip_of() ^ mate(HAND, k)) * plan.part, plan.part), plan.part)
    add = core_of() == (1 if reverse else 0)
    out_ref[...] = piece_ref[...] + jnp.where(add, keep_ref[here, :], 0.0)


def before_kernel(reverse, span, *refs):
    parts, got_ref, base, outs = refs[:4], refs[4], refs[5:-4], refs[-4:]
    chip = chip_of()
    far = lax.rem(lax.axis_index("ctx") // span, 2) == (0 if reverse else 1)
    start = jnp.where(far, got_ref[...], 0.0)
    for more in base:
        start = start + more[...]
    for k in range(QUAD):
        total = start
        for m in range(QUAD):
            here, there = chip ^ mate(GATHER, m), chip ^ mate(HAND, k)
            first = here > there if reverse else here < there
            total = total + jnp.where(first, parts[m][...], 0.0)
        outs[k][...] = total


def swap(x, distance):
    count = lax.axis_size("ctx")
    return lax.ppermute(x, "ctx", [(i, i ^ distance) for i in range(count)])


def quad_swap(x, slot, orders):
    count = lax.axis_size("ctx")
    return lax.ppermute(x, "ctx", [(i, i ^ 2 * orders[i % 2][slot]) for i in range(count)])


def gather_sums(plan, keep, near):
    mine = run(functools.partial(split_kernel, plan), [plan.piece] * QUAD, keep, near)
    return [mine[0]], [quad_swap(mine[k], k, GATHER) for k in range(1, QUAD)]


def across(parts, reverse):
    count = lax.axis_size("ctx")
    total = (parts[0] + parts[1]) + (parts[2] + parts[3])
    held = total
    base = []
    span = 2 * QUAD
    while True:
        got = swap(total, span)
        if 2 * span >= count:
            return held, (got, base, span)
        far = lax.rem(lax.axis_index("ctx") // span, 2) == (0 if reverse else 1)
        term = jnp.where(far, got, 0.0)
        base = [base[0] + term] if base else [term]
        total = total + got
        span *= 2


def hand_out(plan, parts, got, base, span, reverse):
    outs = run(
        functools.partial(before_kernel, reverse, span),
        [plan.piece] * QUAD,
        *parts,
        got,
        *base,
    )
    return outs, [quad_swap(outs[k], k, HAND) for k in range(1, QUAD)]


def carried(plan, sums_of, work, reverse):
    near = swap(sums_of[0, 0], 1)
    keep = sums_of[0, 1]
    own, came = gather_sums(plan, keep, near)
    results = []

    def meanwhile(thunks, held, values):
        done = [t(held) for t in thunks]
        results.extend(done)
        return after(values, done) if done else values

    parts = own + meanwhile(work[0], own[0], came)
    held, (got, base, span) = across(parts, reverse)
    got = meanwhile(work[1], held, got)
    outs, came = hand_out(plan, parts, got, base, span, reverse)
    came = meanwhile(work[2], outs[0], came)
    own = [outs[0]] + came
    pieces = {(0, 1): own + [near]}
    pieces[0, 0] = [
        swap(run(functools.partial(onward_kernel, plan, reverse, k), plan.piece, x, keep), 1)
        for k, x in enumerate(own)
    ]
    return pieces, results


def head_total(sums):
    if lax.axis_size("head") == 2:
        return sums, lax.ppermute(sums, "head", [(0, 1), (1, 0)])
    return lax.psum(sums, "head"), jnp.zeros_like(sums)


def per_device(queries, key_rows, value_rows, gate_rows, cotangent):
    plan = Plan(*queries.shape)
    groups = [(c, side) for c in range(CHUNKS) for side in (0, 1)]
    late = [(c, side) for c in range(CHUNKS) for side in (1, 0)]
    count = len(groups)
    k, v, first_sum = run(
        functools.partial(first_kernel, plan, groups),
        [plan.given, plan.given, plan.tall],
        pltpu.with_memory_space_constraint(key_rows, pltpu.HBM),
        pltpu.with_memory_space_constraint(value_rows, pltpu.HBM),
        scratch=[pltpu.SemaphoreType.DMA((2 * count,))],
        in_specs=[ANY, ANY],
    )
    sums = {groups[0]: first_sum}
    for where in groups[1:]:
        sums[where] = run(functools.partial(next_kernel, plan, where), plan.tall, k, v)

    def local(where):
        def thunk(held):
            args = after((queries, k, v, gate_rows, cotangent), held)
            return run(
                functools.partial(local_kernel, plan, where),
                [plan.low, plan.low, plan.square, plan.full, plan.full],
                *args,
            )

        return thunk

    thunks = [local(where) for where in groups]
    pieces, made = carried(plan, sums, ([], thunks, []), False)
    made = dict(zip(groups, made))
    lq, lk, weights, inside, gated = ({w: made[w][n] for w in groups} for n in range(5))
    state, attended, running = {}, {}, ()
    for n, where in enumerate(late):
        last = n == count - 1
        state[where], attended[where], *running = run(
            functools.partial(attend_kernel, plan, where[1], n == 0, last),
            [plan.state, plan.full] + ([plan.sums] if last else [plan.wide] * 2),
            *pieces[where],
            lq[where],
            inside[where],
            gated[where],
            *running,
        )
    scales = head_total(running[0])
    d_attn, sums = {}, {}
    for n, where in enumerate(groups):
        d_attn[where], sums[where], *more = run(
            functools.partial(grad_kernel, plan, n == 0),
            [plan.low, plan.tall] + ([plan.wide] * 2 if n == 0 else []),
            *scales,
            attended[where],
            gated[where],
            lq[where],
        )
        scales = more or scales
    outer = []

    def inner(where):
        def thunk(held):
            first = not outer
            args = after(
                (
                    state[where], scales[0], weights[where], d_attn[where], lq[where], lk[where],
                    attended[where], gated[where], queries, v, gate_rows,
                ),
                held,
            )
            gq, gg, pk, pv = run(
                functools.partial(inside_kernel, plan, where, first),
                [plan.given, plan.given, plan.full, plan.full],
                *args,
                *outer,
                scratch=[pltpu.VMEM((plan.rows, plan.span), BF16)] * 2
                + [pltpu.SemaphoreType.DMA((2,))],
                in_specs=[VMEM] * 11 + [ANY] * len(outer),
                out_specs=[ANY, ANY, VMEM, VMEM],
                aliases={} if first else {11: 0, 12: 1},
            )
            outer[:] = [gq, gg]
            return pk, pv

        return thunk

    thunks = [inner(where) for where in groups]
    pieces, made = carried(plan, sums, ([], thunks[:1], thunks[1:]), True)
    made = dict(zip(groups, made))
    where = (0, 1)
    state_scratch = pltpu.VMEM((plan.span, DH), BF16)
    ends = run(
        functools.partial(finish_kernel, plan, where),
        [plan.low, plan.low],
        *pieces[where],
        k,
        v,
        lk[where],
        *made[where],
        scratch=[state_scratch],
    )
    where = (0, 0)
    ends = run(
        functools.partial(finish_kernel, plan, where),
        [plan.given, plan.given],
        *pieces[where],
        k,
        v,
        lk[where],
        *made[where],
        *ends,
        scratch=[state_scratch]
        + [pltpu.VMEM((plan.rows, plan.span), BF16)] * 2
        + [pltpu.SemaphoreType.DMA((2 + 2 * plan.group // plan.batch,))],
        in_specs=[VMEM] * 11,
        out_specs=[ANY, ANY],
    )
    return (outer[0], ends[0], ends[1], outer[1])


def solution(mesh):
    spec = P("ctx", "head")
    return jax.shard_map(
        per_device, mesh=mesh, in_specs=(spec,) * 5, out_specs=(spec,) * 4, check_vma=False
    )
```

```python
import functools

import jax
import jax.numpy as jnp
from jax import lax
from jax.experimental import pallas as pl
from jax.experimental.pallas import tpu as pltpu
from jax.sharding import PartitionSpec as P

H = 32
DH = 128
EPSILON = 1e-06
QUAD = 4
SECTIONS = ((1, 2), (3, 0))
GATHER = ((0, 1, 2, 3), (0, 1, 2, 3))
HAND = ((0, 1, 2, 3), (0, 1, 2, 3))
CHUNKS = 1
BATCH = 4
F32 = jnp.float32
BF16 = jnp.bfloat16
SMALL = 16 * 1024 * 1024
LARGE = 60 * 1024 * 1024
ANY = pl.BlockSpec(memory_space=pl.ANY)
VMEM = pl.BlockSpec(memory_space=pltpu.VMEM)


def dot(a, b, ca, cb):
    return lax.dot_general(a, b, (((ca,), (cb,)), ((), ())), preferred_element_type=F32)


def sigmoid(x):
    return 0.5 + 0.5 * jnp.tanh(0.5 * x)


def thirds(x):
    first = x.astype(BF16)
    rest = x - first.astype(F32)
    second = rest.astype(BF16)
    return [first, second, (rest - second.astype(F32)).astype(BF16)]


def chooser(rows, width):
    line = lax.broadcasted_iota(jnp.int32, (rows, width), 0)
    column = lax.broadcasted_iota(jnp.int32, (rows, width), 1)
    return jnp.where(line == column // DH, 1.0, 0.0).astype(BF16)


def core_of():
    return lax.rem(lax.axis_index("ctx"), 2)


def chip_of():
    return lax.rem(lax.axis_index("ctx") // 2, QUAD)


def mate(orders, n, other=0):
    first, second = orders[0][n], orders[1][n]
    return first + (core_of() ^ other) * (second - first)


def head(g):
    return slice(g * DH, (g + 1) * DH)


def after(values, done):
    flat, tree = jax.tree.flatten(values)
    out = lax.optimization_barrier(tuple(flat) + tuple(jax.tree.leaves(done)))
    return jax.tree.unflatten(tree, out[: len(flat)])


class Plan:
    def __init__(self, rows, width):
        self.rows, self.width = rows, width
        self.heads = width // DH
        self.group = self.heads // (2 * CHUNKS)
        self.span = self.group * DH
        self.batch = BATCH if self.group % BATCH == 0 else 1
        self.part = self.span // QUAD
        self.split = self.part % DH == 0
        self.block = jax.ShapeDtypeStruct((2 * self.part, DH), F32)
        self.tall = jax.ShapeDtypeStruct((self.span, DH), F32)
        self.piece = jax.ShapeDtypeStruct((self.part, DH), F32)
        self.low = jax.ShapeDtypeStruct((rows, self.span), BF16)
        self.full = jax.ShapeDtypeStruct((rows, self.span), F32)
        self.wide = jax.ShapeDtypeStruct((rows, DH), F32)
        self.square = jax.ShapeDtypeStruct((self.group, rows, rows), BF16)
        self.state = jax.ShapeDtypeStruct((self.span, DH), BF16)
        self.given = jax.ShapeDtypeStruct((rows, width), BF16)
        self.sums = jax.ShapeDtypeStruct((8, rows), F32)

    def start(self, chunk, side):
        half = lax.rem(core_of() + 1 + side, 2)
        return pl.multiple_of((half * CHUNKS + chunk) * self.span, self.span)

    def columns(self, chunk, side, g=None):
        start = self.start(chunk, side)
        if g is None:
            return pl.ds(start, self.span)
        return pl.ds(pl.multiple_of(start + g * DH, DH), DH)


    def section(self, n):
        count = self.part // DH
        chip = chip_of()
        return [(chip ^ k) * count + h for k in SECTIONS[n] for h in range(count)]

    def own_part(self, k):
        return pl.ds(pl.multiple_of((chip_of() ^ k) * self.part, self.part), self.part)


def run(kernel, out_shape, *args, scratch=(), in_specs=None, out_specs=None, limit=SMALL, aliases=None):
    extra = {}
    if in_specs is not None:
        extra["in_specs"] = in_specs
    if out_specs is not None:
        extra["out_specs"] = out_specs
    if aliases:
        extra["input_output_aliases"] = aliases
    return pl.pallas_call(
        kernel,
        out_shape=out_shape,
        scratch_shapes=list(scratch),
        compiler_params=pltpu.CompilerParams(vmem_limit_bytes=limit),
        **extra,
    )(*args)


def key_state(k, v):
    return dot((k * sigmoid(k)).astype(BF16), v, 0, 0)


def first_kernel(plan, order, k_hbm, v_hbm, k_ref, v_ref, out_ref, sems):
    copies = []
    for n, where in enumerate(order):
        at = (slice(None), plan.columns(*where))
        for m, (source, target) in enumerate(((k_hbm, k_ref), (v_hbm, v_ref))):
            copy = pltpu.make_async_copy(source.at[at], target.at[at], sems.at[2 * n + m])
            copy.start()
            copies.append(copy)
    copies[0].wait()
    copies[1].wait()
    next_kernel(plan, order[0], 0 if plan.split else None, k_ref, v_ref, out_ref)
    for copy in copies[2:]:
        copy.wait()


def next_kernel(plan, where, section, k_ref, v_ref, out_ref):
    heads = range(plan.group) if section is None else plan.section(section)
    for n, g in enumerate(heads):
        at = plan.columns(*where, g)
        out_ref[head(n), :] = key_state(k_ref[:, at].astype(F32), v_ref[:, at])


def causal_mask(rows):
    return lax.broadcasted_iota(jnp.int32, (rows, rows), 0) >= lax.broadcasted_iota(
        jnp.int32, (rows, rows), 1
    )


def key_part(plan, where, k_ref, lk_ref, slope_ref):
    for g in range(plan.group):
        k = k_ref[:, plan.columns(*where, g)].astype(F32)
        sig = sigmoid(k)
        lk_ref[:, head(g)] = (k * sig).astype(BF16)
        slope_ref[:, head(g)] = sig * (1.0 + k * (1.0 - sig))


def early_key_kernel(plan, groups, k_ref, *outs):
    @pl.when(core_of() == 0)
    def _():
        for n, where in enumerate(groups):
            key_part(plan, where, k_ref, *outs[2 * n : 2 * n + 2])


def local_kernel(plan, where, q_ref, k_ref, v_ref, gate_ref, cot_ref, *refs):
    early, keys, (lq_ref, w_ref, att_ref, gated_ref) = refs[:2], refs[2:4], refs[4:]

    @pl.when(core_of() == 0)
    def _():
        for made, out in zip(early, keys):
            out[...] = made[...]

    @pl.when(core_of() == 1)
    def _():
        key_part(plan, where, k_ref, *keys)

    causal = causal_mask(plan.rows)
    for g in range(plan.group):
        at = plan.columns(*where, g)
        q = q_ref[:, at].astype(F32)
        lq = (q * sigmoid(q)).astype(BF16)
        lq_ref[:, head(g)] = lq
        weights = jnp.where(causal, dot(lq, keys[0][:, head(g)], 1, 1), 0.0).astype(BF16)
        w_ref[g] = weights
        att_ref[:, head(g)] = dot(weights, v_ref[:, at], 1, 0)
        gated_ref[:, head(g)] = cot_ref[:, at].astype(F32) * sigmoid(gate_ref[:, at].astype(F32))


def gate_part(plan, where, inv_ref, gate_ref, att_ref, gated_ref, out_ref):
    for g in range(plan.group):
        gate = sigmoid(gate_ref[:, plan.columns(*where, g)].astype(F32))
        normed = att_ref[:, head(g)] * inv_ref[...]
        out_ref[:, head(g)] = (gated_ref[:, head(g)] * normed * (1.0 - gate)).astype(BF16)


def early_gate_kernel(plan, groups, inv_ref, gate_ref, *refs):
    count = len(groups)

    @pl.when(core_of() == 0)
    def _():
        for n, where in enumerate(groups):
            att_ref, gated_ref, out_ref = refs[n::count]
            gate_part(plan, where, inv_ref, gate_ref, att_ref, gated_ref, out_ref)


def place_state(plan, reverse, side, pieces, add_ref, state_ref):
    add = core_of() == (0 if reverse else 1)
    for slot in range(QUAD):
        k = mate(HAND, slot, 1 - side)
        piece = pieces[slot][...]
        if add_ref:
            piece = piece + jnp.where(add, near_part(plan, add_ref, k), 0.0)
        state_ref[plan.own_part(k), :] = piece.astype(BF16)


def near_part(plan, refs, k):
    if len(refs) == 1:
        return refs[0][plan.own_part(k), :]
    place = lax.rem(k + QUAD - 1, QUAD)
    here = pl.ds(pl.multiple_of(lax.rem(place, 2) * plan.part, plan.part), plan.part)
    return jnp.where(place < 2, refs[0][here, :], refs[1][here, :])


def attend_kernel(plan, side, first, last, *refs):
    extra = side * (1 + plan.split)
    pieces, add_ref = refs[:4], refs[4 : 4 + extra]
    refs = refs[4 + extra :]
    lq_ref, local_ref, gated_ref = refs[:3]
    refs = refs[3:]
    if not first:
        square, inner = refs[0][...], refs[1][...]
        refs = refs[2:]
    state_ref, att_ref = refs[:2]
    place_state(plan, False, side, pieces, add_ref, state_ref)
    for g in range(plan.group):
        att = local_ref[:, head(g)] + dot(lq_ref[:, head(g)], state_ref[head(g), :], 1, 0)
        att_ref[:, head(g)] = att
        if first and g == 0:
            square, inner = att * att, gated_ref[:, head(g)] * att
        else:
            square, inner = square + att * att, inner + gated_ref[:, head(g)] * att
    if last:
        pick = chooser(8, 2 * DH)
        terms = thirds(jnp.concatenate([square, inner], axis=1))
        refs[2][...] = sum(dot(pick, term, 1, 1) for term in terms)
    else:
        refs[2][...] = square
        refs[3][...] = inner


def section_kernel(plan, n, lq_ref, d_ref, sum_ref):
    for place, g in enumerate(plan.section(n)):
        at = pl.ds(pl.multiple_of(g * DH, DH), DH)
        sum_ref[head(place), :] = dot(lq_ref[:, at], d_ref[:, at], 0, 0)


def grad_kernel(plan, first, a_ref, b_ref, att_ref, gated_ref, lq_ref, d_ref, sum_ref, *more):
    if first:
        total = a_ref[...] + b_ref[...]
        sumsq, raw = total[0:1, :], total[1:2, :]
        inv = 1.0 / jnp.sqrt(sumsq * (1.0 / (H * DH)) + EPSILON)
        coef = raw * inv * (1.0 / (H * DH)) * inv * inv
        line = lax.broadcasted_iota(jnp.int32, total.shape, 0)
        rows = jnp.where(line == 0, inv, jnp.where(line == 1, coef, 0.0))
        pick = chooser(8, 2 * DH)
        both = sum(dot(term, pick, 0, 0) for term in thirds(rows))
        inv, coef = both[:, :DH], both[:, DH:]
        more[0][...] = inv
        more[1][...] = coef
    else:
        inv, coef = a_ref[...], b_ref[...]
    for g in range(plan.group):
        d = (gated_ref[:, head(g)] * inv - att_ref[:, head(g)] * coef).astype(BF16)
        d_ref[:, head(g)] = d
        if not (first and plan.split):
            sum_ref[head(g), :] = dot(lq_ref[:, head(g)], d, 0, 0)
    if first and plan.split:
        section_kernel(plan, 0, lq_ref, d_ref, sum_ref)


def inside_kernel(plan, where, first, *refs):
    (state_ref, inv_ref, w_ref, d_ref, lq_ref, lk_ref, att_ref, gated_ref) = refs[:8]
    q_ref, v_ref, gate_ref, early_ref = refs[8:12]
    gq_hbm, gg_hbm, pk_ref, pv_ref, gq, gg, sems = refs[12 if first else 14 :]

    @pl.when(core_of() == 0)
    def _():
        gg[...] = early_ref[...]

    @pl.when(core_of() == 1)
    def _():
        gate_part(plan, where, inv_ref, gate_ref, att_ref, gated_ref, gg)

    causal = causal_mask(plan.rows)
    for g in range(plan.group):
        at = plan.columns(*where, g)
        d = d_ref[:, head(g)]
        dw = jnp.where(causal, dot(d, v_ref[:, at], 1, 1), 0.0).astype(BF16)
        glq = dot(dw, lk_ref[:, head(g)], 1, 0) + dot(d, state_ref[head(g), :], 1, 1)
        q = q_ref[:, at].astype(F32)
        sig = sigmoid(q)
        gq[:, head(g)] = (glq * (sig * (1.0 + q * (1.0 - sig)))).astype(BF16)
        pk_ref[:, head(g)] = dot(dw, lq_ref[:, head(g)], 0, 0)
        pv_ref[:, head(g)] = dot(w_ref[g], d, 0, 0)
    send_out(plan, where, ((gq, gq_hbm), (gg, gg_hbm)), sems)


def send_out(plan, where, pairs, sems):
    at = (slice(None), plan.columns(*where))
    copies = [
        pltpu.make_async_copy(source, target.at[at], sems.at[n])
        for n, (source, target) in enumerate(pairs)
    ]
    for copy in copies:
        copy.start()
    for copy in copies:
        copy.wait()


def finish_kernel(plan, where, *refs):
    side = where[1]
    extra = side * (1 + plan.split)
    pieces, add_ref = refs[:4], refs[4 : 4 + extra]
    refs = refs[4 + extra :]
    slope_ref, v_ref, lk_ref, pk_ref, pv_ref = refs[:5]
    if side:
        gk, gv, state_ref = refs[5:]
    else:
        gk_done, gv_done, gk_hbm, gv_hbm, state_ref, gk, gv, sems = refs[5:]
    copies = []

    def send(pairs, at):
        for source, target in pairs:
            copy = pltpu.make_async_copy(source, target.at[:, at], sems.at[len(copies)])
            copy.start()
            copies.append(copy)

    if not side:
        send(((gk_done, gk_hbm), (gv_done, gv_hbm)), plan.columns(where[0], 1))
    place_state(plan, True, side, pieces, add_ref, state_ref)
    for g in range(plan.group):
        at = plan.columns(*where, g)
        state = state_ref[head(g), :]
        gv[:, head(g)] = (pv_ref[:, head(g)] + dot(lk_ref[:, head(g)], state, 1, 0)).astype(BF16)
        glk = pk_ref[:, head(g)] + dot(v_ref[:, at], state, 1, 1)
        gk[:, head(g)] = (glk * slope_ref[:, head(g)]).astype(BF16)
        if not side and (g + 1) % plan.batch == 0:
            first = g + 1 - plan.batch
            here = slice(first * DH, (g + 1) * DH)
            start = pl.multiple_of(plan.start(*where) + first * DH, DH)
            pairs = ((gk.at[:, here], gk_hbm), (gv.at[:, here], gv_hbm))
            send(pairs, pl.ds(start, plan.batch * DH))
    for copy in copies:
        copy.wait()


def split_kernel(plan, slots, keep_ref, got_ref, *outs):
    for n, slot in enumerate(slots):
        k = mate(GATHER, slot)
        if len(slots) == QUAD:
            here = plan.own_part(k)
        else:
            here = pl.ds(pl.multiple_of(lax.rem(k + 1, 2) * plan.part, plan.part), plan.part)
        outs[n][...] = keep_ref[plan.own_part(k), :] + got_ref[here, :]


def onward_kernel(plan, reverse, k, piece_ref, keep_ref, out_ref):
    add = core_of() == (1 if reverse else 0)
    out_ref[...] = piece_ref[...] + jnp.where(add, keep_ref[plan.own_part(mate(HAND, k)), :], 0.0)


def before_kernel(reverse, span, *refs):
    parts, got_ref, base, outs = refs[:4], refs[4], refs[5:-4], refs[-4:]
    chip = chip_of()
    far = lax.rem(lax.axis_index("ctx") // span, 2) == (0 if reverse else 1)
    start = jnp.where(far, got_ref[...], 0.0)
    for more in base:
        start = start + more[...]
    for k in range(QUAD):
        total = start
        for m in range(QUAD):
            here, there = chip ^ mate(GATHER, m), chip ^ mate(HAND, k)
            first = here > there if reverse else here < there
            total = total + jnp.where(first, parts[m][...], 0.0)
        outs[k][...] = total


def swap(x, distance):
    count = lax.axis_size("ctx")
    return lax.ppermute(x, "ctx", [(i, i ^ distance) for i in range(count)])


def quad_swap(x, slot, orders):
    count = lax.axis_size("ctx")
    return lax.ppermute(x, "ctx", [(i, i ^ 2 * orders[i % 2][slot]) for i in range(count)])


def gather_sums(plan, keep, near, early):
    first = after(near[0], early(near[0]))
    mine, came = {}, {}
    for slots, got in zip(SECTIONS if plan.split else [range(QUAD)], [first] + near[1:]):
        keep, got = after((keep, got), mine)
        made = run(
            functools.partial(split_kernel, plan, slots), [plan.piece] * len(slots), keep, got
        )
        for slot, x in zip(slots, made):
            mine[slot] = x
            if slot:
                came[slot] = quad_swap(x, slot, GATHER)
    return [mine[0]], [came[slot] for slot in range(1, QUAD)]


def across(parts, reverse):
    count = lax.axis_size("ctx")
    total = (parts[0] + parts[1]) + (parts[2] + parts[3])
    held = total
    base = []
    span = 2 * QUAD
    while True:
        got = swap(total, span)
        if 2 * span >= count:
            return held, (got, base, span)
        far = lax.rem(lax.axis_index("ctx") // span, 2) == (0 if reverse else 1)
        term = jnp.where(far, got, 0.0)
        base = [base[0] + term] if base else [term]
        total = total + got
        span *= 2


def hand_out(plan, parts, got, base, span, reverse):
    outs = run(
        functools.partial(before_kernel, reverse, span),
        [plan.piece] * QUAD,
        *parts,
        got,
        *base,
    )
    return outs, [quad_swap(outs[k], k, HAND) for k in range(1, QUAD)]


def carried(plan, sums_of, early, work, reverse):
    near = [swap(x, 1) for x in sums_of[0, 0]]
    keep = sums_of[0, 1]
    own, came = gather_sums(plan, keep, near, early)
    results = []

    def meanwhile(thunks, held, values):
        done = [t(held) for t in thunks]
        results.extend(done)
        return after(values, done) if done else values

    parts = own + meanwhile(work[0], own[0], came)
    held, (got, base, span) = across(parts, reverse)
    got = meanwhile(work[1], held, got)
    outs, came = hand_out(plan, parts, got, base, span, reverse)
    came = meanwhile(work[2], outs[0], came)
    own = [outs[0]] + came
    pieces = {(0, 1): own + near}
    pieces[0, 0] = [
        swap(run(functools.partial(onward_kernel, plan, reverse, k), plan.piece, x, keep), 1)
        for k, x in enumerate(own)
    ]
    return pieces, results


def head_total(sums):
    if lax.axis_size("head") == 2:
        return sums, lax.ppermute(sums, "head", [(0, 1), (1, 0)])
    return lax.psum(sums, "head"), jnp.zeros_like(sums)


def per_device(queries, key_rows, value_rows, gate_rows, cotangent):
    plan = Plan(*queries.shape)
    groups = [(c, side) for c in range(CHUNKS) for side in (0, 1)]
    late = [(c, side) for c in range(CHUNKS) for side in (1, 0)]
    count = len(groups)
    k, v, first_sum = run(
        functools.partial(first_kernel, plan, groups),
        [plan.given, plan.given, plan.block if plan.split else plan.tall],
        pltpu.with_memory_space_constraint(key_rows, pltpu.HBM),
        pltpu.with_memory_space_constraint(value_rows, pltpu.HBM),
        scratch=[pltpu.SemaphoreType.DMA((2 * count,))],
        in_specs=[ANY, ANY],
    )
    sums = {groups[0]: [first_sum]}
    if plan.split:
        second = functools.partial(next_kernel, plan, groups[0], 1)
        sums[groups[0]].append(run(second, plan.block, k, v))
    sums[groups[1]] = run(functools.partial(next_kernel, plan, groups[1], None), plan.tall, k, v)

    ahead = []

    def early(held):
        kernel = functools.partial(early_key_kernel, plan, groups)
        ahead[:] = run(kernel, [plan.low, plan.full] * count, after(k, held))
        return ahead

    def local(where):
        def thunk(held):
            n = 2 * groups.index(where)
            args = after((queries, k, v, gate_rows, cotangent), held)
            return run(
                functools.partial(local_kernel, plan, where),
                [plan.low, plan.full, plan.low, plan.square, plan.full, plan.full],
                *args,
                *ahead[n : n + 2],
            )

        return thunk

    thunks = [local(where) for where in groups]
    pieces, made = carried(plan, sums, early, ([], thunks, []), False)
    made = dict(zip(groups, made))
    lk, slope, lq, weights, inside, gated = ({w: made[w][n] for w in groups} for n in range(6))
    state, attended, running = {}, {}, ()
    for n, where in enumerate(late):
        last = n == count - 1
        state[where], attended[where], *running = run(
            functools.partial(attend_kernel, plan, where[1], n == 0, last),
            [plan.state, plan.full] + ([plan.sums] if last else [plan.wide] * 2),
            *pieces[where],
            lq[where],
            inside[where],
            gated[where],
            *running,
        )
    scales = head_total(running[0])
    d_attn, sums = {}, {}
    for n, where in enumerate(groups):
        total = plan.block if n == 0 and plan.split else plan.tall
        d_attn[where], sums[where], *more = run(
            functools.partial(grad_kernel, plan, n == 0),
            [plan.low, total] + ([plan.wide] * 2 if n == 0 else []),
            *scales,
            attended[where],
            gated[where],
            lq[where],
        )
        scales = more or scales
        if n == 0:
            sums[where] = [sums[where]]
            if plan.split:
                second = functools.partial(section_kernel, plan, 1)
                sums[where].append(run(second, plan.block, lq[where], d_attn[where]))
    gates = []

    def early_gates(held):
        args = (scales[0], gate_rows, *(attended[w] for w in groups), *(gated[w] for w in groups))
        kernel = functools.partial(early_gate_kernel, plan, groups)
        gates[:] = run(kernel, [plan.low] * count, *after(args, held))
        return gates

    outer = []

    def inner(where):
        def thunk(held):
            first = not outer
            args = after(
                (
                    state[where], scales[0], weights[where], d_attn[where], lq[where], lk[where],
                    attended[where], gated[where], queries, v, gate_rows,
                    gates[groups.index(where)],
                ),
                held,
            )
            gq, gg, pk, pv = run(
                functools.partial(inside_kernel, plan, where, first),
                [plan.given, plan.given, plan.full, plan.full],
                *args,
                *outer,
                scratch=[pltpu.VMEM((plan.rows, plan.span), BF16)] * 2
                + [pltpu.SemaphoreType.DMA((2,))],
                in_specs=[VMEM] * 12 + [ANY] * len(outer),
                out_specs=[ANY, ANY, VMEM, VMEM],
                aliases={} if first else {12: 0, 13: 1},
            )
            outer[:] = [gq, gg]
            return pk, pv

        return thunk

    thunks = [inner(where) for where in groups]
    pieces, made = carried(plan, sums, early_gates, ([], thunks[:1], thunks[1:]), True)
    made = dict(zip(groups, made))
    where = (0, 1)
    state_scratch = pltpu.VMEM((plan.span, DH), BF16)
    ends = run(
        functools.partial(finish_kernel, plan, where),
        [plan.low, plan.low],
        *pieces[where],
        slope[where],
        v,
        lk[where],
        *made[where],
        scratch=[state_scratch],
    )
    where = (0, 0)
    ends = run(
        functools.partial(finish_kernel, plan, where),
        [plan.given, plan.given],
        *pieces[where],
        slope[where],
        v,
        lk[where],
        *made[where],
        *ends,
        scratch=[state_scratch]
        + [pltpu.VMEM((plan.rows, plan.span), BF16)] * 2
        + [pltpu.SemaphoreType.DMA((2 + 2 * plan.group // plan.batch,))],
        in_specs=[VMEM] * 11,
        out_specs=[ANY, ANY],
    )
    return (outer[0], ends[0], ends[1], outer[1])


def solution(mesh):
    spec = P("ctx", "head")
    return jax.shard_map(
        per_device, mesh=mesh, in_specs=(spec,) * 5, out_specs=(spec,) * 4, check_vma=False
    )
```

```python
import functools

import jax
import jax.numpy as jnp
from jax import lax
from jax.experimental import pallas as pl
from jax.experimental.pallas import tpu as pltpu
from jax.sharding import PartitionSpec as P

H = 32
DH = 128
EPSILON = 1e-06
QUAD = 4
SECTIONS = ((1, 2), (3, 0))
GATHER = ((0, 1, 2, 3), (0, 1, 2, 3))
HAND = ((0, 1, 2, 3), (0, 3, 1, 2))
CHUNKS = 1
BATCH = 4
F32 = jnp.float32
BF16 = jnp.bfloat16
SMALL = 16 * 1024 * 1024
LARGE = 60 * 1024 * 1024
ANY = pl.BlockSpec(memory_space=pl.ANY)
VMEM = pl.BlockSpec(memory_space=pltpu.VMEM)


def dot(a, b, ca, cb):
    return lax.dot_general(a, b, (((ca,), (cb,)), ((), ())), preferred_element_type=F32)


def sigmoid(x):
    return 0.5 + 0.5 * jnp.tanh(0.5 * x)


def thirds(x):
    first = x.astype(BF16)
    rest = x - first.astype(F32)
    second = rest.astype(BF16)
    return [first, second, (rest - second.astype(F32)).astype(BF16)]


def chooser(rows, width):
    line = lax.broadcasted_iota(jnp.int32, (rows, width), 0)
    column = lax.broadcasted_iota(jnp.int32, (rows, width), 1)
    return jnp.where(line == column // DH, 1.0, 0.0).astype(BF16)


def core_of():
    return lax.rem(lax.axis_index("ctx"), 2)


def chip_of():
    return lax.rem(lax.axis_index("ctx") // 2, QUAD)


def mate(orders, n, other=0):
    first, second = orders[0][n], orders[1][n]
    return first + (core_of() ^ other) * (second - first)


def head(g):
    return slice(g * DH, (g + 1) * DH)


def after(values, done):
    flat, tree = jax.tree.flatten(values)
    out = lax.optimization_barrier(tuple(flat) + tuple(jax.tree.leaves(done)))
    return jax.tree.unflatten(tree, out[: len(flat)])


class Plan:
    def __init__(self, rows, width):
        self.rows, self.width = rows, width
        self.heads = width // DH
        self.group = self.heads // (2 * CHUNKS)
        self.span = self.group * DH
        self.batch = BATCH if self.group % BATCH == 0 else 1
        self.part = self.span // QUAD
        self.split = self.part % DH == 0
        self.block = jax.ShapeDtypeStruct((2 * self.part, DH), F32)
        self.tall = jax.ShapeDtypeStruct((self.span, DH), F32)
        self.piece = jax.ShapeDtypeStruct((self.part, DH), F32)
        self.low = jax.ShapeDtypeStruct((rows, self.span), BF16)
        self.full = jax.ShapeDtypeStruct((rows, self.span), F32)
        self.wide = jax.ShapeDtypeStruct((rows, DH), F32)
        self.square = jax.ShapeDtypeStruct((self.group, rows, rows), BF16)
        self.state = jax.ShapeDtypeStruct((self.span, DH), BF16)
        self.given = jax.ShapeDtypeStruct((rows, width), BF16)
        self.sums = jax.ShapeDtypeStruct((8, rows), F32)

    def start(self, chunk, side):
        half = lax.rem(core_of() + 1 + side, 2)
        return pl.multiple_of((half * CHUNKS + chunk) * self.span, self.span)

    def columns(self, chunk, side, g=None):
        start = self.start(chunk, side)
        if g is None:
            return pl.ds(start, self.span)
        return pl.ds(pl.multiple_of(start + g * DH, DH), DH)


    def section(self, n):
        count = self.part // DH
        chip = chip_of()
        return [(chip ^ k) * count + h for k in SECTIONS[n] for h in range(count)]

    def own_part(self, k):
        return pl.ds(pl.multiple_of((chip_of() ^ k) * self.part, self.part), self.part)


def run(kernel, out_shape, *args, scratch=(), in_specs=None, out_specs=None, limit=SMALL, aliases=None):
    extra = {}
    if in_specs is not None:
        extra["in_specs"] = in_specs
    if out_specs is not None:
        extra["out_specs"] = out_specs
    if aliases:
        extra["input_output_aliases"] = aliases
    return pl.pallas_call(
        kernel,
        out_shape=out_shape,
        scratch_shapes=list(scratch),
        compiler_params=pltpu.CompilerParams(vmem_limit_bytes=limit),
        **extra,
    )(*args)


def key_state(k, v):
    return dot((k * sigmoid(k)).astype(BF16), v, 0, 0)


def first_kernel(plan, order, k_hbm, v_hbm, k_ref, v_ref, out_ref, sems):
    copies = []
    for n, where in enumerate(order):
        at = (slice(None), plan.columns(*where))
        for m, (source, target) in enumerate(((k_hbm, k_ref), (v_hbm, v_ref))):
            copy = pltpu.make_async_copy(source.at[at], target.at[at], sems.at[2 * n + m])
            copy.start()
            copies.append(copy)
    copies[0].wait()
    copies[1].wait()
    next_kernel(plan, order[0], 0 if plan.split else None, k_ref, v_ref, out_ref)
    for copy in copies[2:]:
        copy.wait()


def next_kernel(plan, where, section, k_ref, v_ref, out_ref):
    heads = range(plan.group) if section is None else plan.section(section)
    for n, g in enumerate(heads):
        at = plan.columns(*where, g)
        out_ref[head(n), :] = key_state(k_ref[:, at].astype(F32), v_ref[:, at])


def causal_mask(rows):
    return lax.broadcasted_iota(jnp.int32, (rows, rows), 0) >= lax.broadcasted_iota(
        jnp.int32, (rows, rows), 1
    )


def key_part(plan, where, k_ref, lk_ref, slope_ref):
    for g in range(plan.group):
        k = k_ref[:, plan.columns(*where, g)].astype(F32)
        sig = sigmoid(k)
        lk_ref[:, head(g)] = (k * sig).astype(BF16)
        slope_ref[:, head(g)] = sig * (1.0 + k * (1.0 - sig))


def early_key_kernel(plan, groups, k_ref, *outs):
    @pl.when(core_of() == 0)
    def _():
        for n, where in enumerate(groups):
            key_part(plan, where, k_ref, *outs[2 * n : 2 * n + 2])


def local_kernel(plan, where, q_ref, k_ref, v_ref, gate_ref, cot_ref, *refs):
    early, keys, (lq_ref, w_ref, att_ref, gated_ref) = refs[:2], refs[2:4], refs[4:]

    @pl.when(core_of() == 0)
    def _():
        for made, out in zip(early, keys):
            out[...] = made[...]

    @pl.when(core_of() == 1)
    def _():
        key_part(plan, where, k_ref, *keys)

    causal = causal_mask(plan.rows)
    for g in range(plan.group):
        at = plan.columns(*where, g)
        q = q_ref[:, at].astype(F32)
        lq = (q * sigmoid(q)).astype(BF16)
        lq_ref[:, head(g)] = lq
        weights = jnp.where(causal, dot(lq, keys[0][:, head(g)], 1, 1), 0.0).astype(BF16)
        w_ref[g] = weights
        att_ref[:, head(g)] = dot(weights, v_ref[:, at], 1, 0)
        gated_ref[:, head(g)] = cot_ref[:, at].astype(F32) * sigmoid(gate_ref[:, at].astype(F32))


def gate_part(plan, where, inv_ref, gate_ref, att_ref, gated_ref, out_ref):
    for g in range(plan.group):
        gate = sigmoid(gate_ref[:, plan.columns(*where, g)].astype(F32))
        normed = att_ref[:, head(g)] * inv_ref[...]
        out_ref[:, head(g)] = (gated_ref[:, head(g)] * normed * (1.0 - gate)).astype(BF16)


def early_gate_kernel(plan, groups, inv_ref, gate_ref, *refs):
    count = len(groups)

    @pl.when(core_of() == 0)
    def _():
        for n, where in enumerate(groups):
            att_ref, gated_ref, out_ref = refs[n::count]
            gate_part(plan, where, inv_ref, gate_ref, att_ref, gated_ref, out_ref)


def place_state(plan, reverse, side, pieces, add_ref, state_ref):
    add = core_of() == (0 if reverse else 1)
    for slot in range(QUAD):
        k = mate(HAND, slot, 1 - side)
        piece = pieces[slot][...]
        if add_ref:
            piece = piece + jnp.where(add, near_part(plan, add_ref, k), 0.0)
        state_ref[plan.own_part(k), :] = piece.astype(BF16)


def near_part(plan, refs, k):
    if len(refs) == 1:
        return refs[0][plan.own_part(k), :]
    place = lax.rem(k + QUAD - 1, QUAD)
    here = pl.ds(pl.multiple_of(lax.rem(place, 2) * plan.part, plan.part), plan.part)
    return jnp.where(place < 2, refs[0][here, :], refs[1][here, :])


def attend_kernel(plan, side, first, last, *refs):
    extra = side * (1 + plan.split)
    pieces, add_ref = refs[:4], refs[4 : 4 + extra]
    refs = refs[4 + extra :]
    lq_ref, local_ref, gated_ref = refs[:3]
    refs = refs[3:]
    if not first:
        square, inner = refs[0][...], refs[1][...]
        refs = refs[2:]
    state_ref, att_ref = refs[:2]
    place_state(plan, False, side, pieces, add_ref, state_ref)
    for g in range(plan.group):
        att = local_ref[:, head(g)] + dot(lq_ref[:, head(g)], state_ref[head(g), :], 1, 0)
        att_ref[:, head(g)] = att
        if first and g == 0:
            square, inner = att * att, gated_ref[:, head(g)] * att
        else:
            square, inner = square + att * att, inner + gated_ref[:, head(g)] * att
    if last:
        pick = chooser(8, 2 * DH)
        terms = thirds(jnp.concatenate([square, inner], axis=1))
        refs[2][...] = sum(dot(pick, term, 1, 1) for term in terms)
    else:
        refs[2][...] = square
        refs[3][...] = inner


def section_kernel(plan, n, lq_ref, d_ref, sum_ref):
    for place, g in enumerate(plan.section(n)):
        at = pl.ds(pl.multiple_of(g * DH, DH), DH)
        sum_ref[head(place), :] = dot(lq_ref[:, at], d_ref[:, at], 0, 0)


def grad_kernel(plan, first, a_ref, b_ref, att_ref, gated_ref, lq_ref, d_ref, sum_ref, *more):
    if first:
        total = a_ref[...] + b_ref[...]
        sumsq, raw = total[0:1, :], total[1:2, :]
        inv = 1.0 / jnp.sqrt(sumsq * (1.0 / (H * DH)) + EPSILON)
        coef = raw * inv * (1.0 / (H * DH)) * inv * inv
        line = lax.broadcasted_iota(jnp.int32, total.shape, 0)
        rows = jnp.where(line == 0, inv, jnp.where(line == 1, coef, 0.0))
        pick = chooser(8, 2 * DH)
        both = sum(dot(term, pick, 0, 0) for term in thirds(rows))
        inv, coef = both[:, :DH], both[:, DH:]
        more[0][...] = inv
        more[1][...] = coef
    else:
        inv, coef = a_ref[...], b_ref[...]
    for g in range(plan.group):
        d = (gated_ref[:, head(g)] * inv - att_ref[:, head(g)] * coef).astype(BF16)
        d_ref[:, head(g)] = d
        if not (first and plan.split):
            sum_ref[head(g), :] = dot(lq_ref[:, head(g)], d, 0, 0)
    if first and plan.split:
        section_kernel(plan, 0, lq_ref, d_ref, sum_ref)


def inside_kernel(plan, where, first, *refs):
    (state_ref, inv_ref, w_ref, d_ref, lq_ref, lk_ref, att_ref, gated_ref) = refs[:8]
    q_ref, v_ref, gate_ref, early_ref = refs[8:12]
    gq_hbm, gg_hbm, pk_ref, pv_ref, gq, gg, sems = refs[12 if first else 14 :]

    @pl.when(core_of() == 0)
    def _():
        gg[...] = early_ref[...]

    @pl.when(core_of() == 1)
    def _():
        gate_part(plan, where, inv_ref, gate_ref, att_ref, gated_ref, gg)

    causal = causal_mask(plan.rows)
    for g in range(plan.group):
        at = plan.columns(*where, g)
        d = d_ref[:, head(g)]
        dw = jnp.where(causal, dot(d, v_ref[:, at], 1, 1), 0.0).astype(BF16)
        glq = dot(dw, lk_ref[:, head(g)], 1, 0) + dot(d, state_ref[head(g), :], 1, 1)
        q = q_ref[:, at].astype(F32)
        sig = sigmoid(q)
        gq[:, head(g)] = (glq * (sig * (1.0 + q * (1.0 - sig)))).astype(BF16)
        pk_ref[:, head(g)] = dot(dw, lq_ref[:, head(g)], 0, 0)
        pv_ref[:, head(g)] = dot(w_ref[g], d, 0, 0)
    send_out(plan, where, ((gq, gq_hbm), (gg, gg_hbm)), sems)


def send_out(plan, where, pairs, sems):
    at = (slice(None), plan.columns(*where))
    copies = [
        pltpu.make_async_copy(source, target.at[at], sems.at[n])
        for n, (source, target) in enumerate(pairs)
    ]
    for copy in copies:
        copy.start()
    for copy in copies:
        copy.wait()


def finish_kernel(plan, where, *refs):
    side = where[1]
    extra = side * (1 + plan.split)
    pieces, add_ref = refs[:4], refs[4 : 4 + extra]
    refs = refs[4 + extra :]
    slope_ref, v_ref, lk_ref, pk_ref, pv_ref = refs[:5]
    if side:
        gk, gv, state_ref = refs[5:]
    else:
        gk_done, gv_done, gk_hbm, gv_hbm, state_ref, gk, gv, sems = refs[5:]
    copies = []

    def send(pairs, at):
        for source, target in pairs:
            copy = pltpu.make_async_copy(source, target.at[:, at], sems.at[len(copies)])
            copy.start()
            copies.append(copy)

    if not side:
        send(((gk_done, gk_hbm), (gv_done, gv_hbm)), plan.columns(where[0], 1))
    place_state(plan, True, side, pieces, add_ref, state_ref)
    for g in range(plan.group):
        at = plan.columns(*where, g)
        state = state_ref[head(g), :]
        gv[:, head(g)] = (pv_ref[:, head(g)] + dot(lk_ref[:, head(g)], state, 1, 0)).astype(BF16)
        glk = pk_ref[:, head(g)] + dot(v_ref[:, at], state, 1, 1)
        gk[:, head(g)] = (glk * slope_ref[:, head(g)]).astype(BF16)
        if not side and (g + 1) % plan.batch == 0:
            first = g + 1 - plan.batch
            here = slice(first * DH, (g + 1) * DH)
            start = pl.multiple_of(plan.start(*where) + first * DH, DH)
            pairs = ((gk.at[:, here], gk_hbm), (gv.at[:, here], gv_hbm))
            send(pairs, pl.ds(start, plan.batch * DH))
    for copy in copies:
        copy.wait()


def split_kernel(plan, slots, keep_ref, got_ref, *outs):
    for n, slot in enumerate(slots):
        k = mate(GATHER, slot)
        if len(slots) == QUAD:
            here = plan.own_part(k)
        else:
            here = pl.ds(pl.multiple_of(lax.rem(k + 1, 2) * plan.part, plan.part), plan.part)
        outs[n][...] = keep_ref[plan.own_part(k), :] + got_ref[here, :]


def onward_kernel(plan, reverse, k, piece_ref, keep_ref, out_ref):
    add = core_of() == (1 if reverse else 0)
    out_ref[...] = piece_ref[...] + jnp.where(add, keep_ref[plan.own_part(mate(HAND, k)), :], 0.0)


def before_kernel(reverse, span, *refs):
    parts, got_ref, base, outs = refs[:4], refs[4], refs[5:-4], refs[-4:]
    chip = chip_of()
    far = lax.rem(lax.axis_index("ctx") // span, 2) == (0 if reverse else 1)
    start = jnp.where(far, got_ref[...], 0.0)
    for more in base:
        start = start + more[...]
    for k in range(QUAD):
        total = start
        for m in range(QUAD):
            here, there = chip ^ mate(GATHER, m), chip ^ mate(HAND, k)
            first = here > there if reverse else here < there
            total = total + jnp.where(first, parts[m][...], 0.0)
        outs[k][...] = total


def swap(x, distance):
    count = lax.axis_size("ctx")
    return lax.ppermute(x, "ctx", [(i, i ^ distance) for i in range(count)])


def quad_swap(x, slot, orders):
    count = lax.axis_size("ctx")
    return lax.ppermute(x, "ctx", [(i, i ^ 2 * orders[i % 2][slot]) for i in range(count)])


def gather_sums(plan, keep, near, early):
    first = after(near[0], early(near[0]))
    mine, came = {}, {}
    for slots, got in zip(SECTIONS if plan.split else [range(QUAD)], [first] + near[1:]):
        keep, got = after((keep, got), mine)
        made = run(
            functools.partial(split_kernel, plan, slots), [plan.piece] * len(slots), keep, got
        )
        for slot, x in zip(slots, made):
            mine[slot] = x
            if slot:
                came[slot] = quad_swap(x, slot, GATHER)
    return [mine[0]], [came[slot] for slot in range(1, QUAD)]


def across(parts, reverse):
    count = lax.axis_size("ctx")
    total = (parts[0] + parts[1]) + (parts[2] + parts[3])
    held = total
    base = []
    span = 2 * QUAD
    while True:
        got = swap(total, span)
        if 2 * span >= count:
            return held, (got, base, span)
        far = lax.rem(lax.axis_index("ctx") // span, 2) == (0 if reverse else 1)
        term = jnp.where(far, got, 0.0)
        base = [base[0] + term] if base else [term]
        total = total + got
        span *= 2


def hand_out(plan, parts, got, base, span, reverse):
    outs = run(
        functools.partial(before_kernel, reverse, span),
        [plan.piece] * QUAD,
        *parts,
        got,
        *base,
    )
    return outs, [quad_swap(outs[k], k, HAND) for k in range(1, QUAD)]


def carried(plan, sums_of, early, work, reverse):
    near = [swap(x, 1) for x in sums_of[0, 0]]
    keep = sums_of[0, 1]
    own, came = gather_sums(plan, keep, near, early)
    results = []

    def meanwhile(thunks, held, values):
        done = [t(held) for t in thunks]
        results.extend(done)
        return after(values, done) if done else values

    parts = own + meanwhile(work[0], own[0], came)
    held, (got, base, span) = across(parts, reverse)
    got = meanwhile(work[1], held, got)
    outs, came = hand_out(plan, parts, got, base, span, reverse)
    came = meanwhile(work[2], outs[0], came)
    own = [outs[0]] + came
    pieces = {(0, 1): own + near}
    pieces[0, 0] = [
        swap(run(functools.partial(onward_kernel, plan, reverse, k), plan.piece, x, keep), 1)
        for k, x in enumerate(own)
    ]
    return pieces, results


def head_total(sums):
    if lax.axis_size("head") == 2:
        return sums, lax.ppermute(sums, "head", [(0, 1), (1, 0)])
    return lax.psum(sums, "head"), jnp.zeros_like(sums)


def per_device(queries, key_rows, value_rows, gate_rows, cotangent):
    plan = Plan(*queries.shape)
    groups = [(c, side) for c in range(CHUNKS) for side in (0, 1)]
    late = [(c, side) for c in range(CHUNKS) for side in (1, 0)]
    count = len(groups)
    k, v, first_sum = run(
        functools.partial(first_kernel, plan, groups),
        [plan.given, plan.given, plan.block if plan.split else plan.tall],
        pltpu.with_memory_space_constraint(key_rows, pltpu.HBM),
        pltpu.with_memory_space_constraint(value_rows, pltpu.HBM),
        scratch=[pltpu.SemaphoreType.DMA((2 * count,))],
        in_specs=[ANY, ANY],
    )
    sums = {groups[0]: [first_sum]}
    if plan.split:
        second = functools.partial(next_kernel, plan, groups[0], 1)
        sums[groups[0]].append(run(second, plan.block, k, v))
    sums[groups[1]] = run(functools.partial(next_kernel, plan, groups[1], None), plan.tall, k, v)

    ahead = []

    def early(held):
        kernel = functools.partial(early_key_kernel, plan, groups)
        ahead[:] = run(kernel, [plan.low, plan.full] * count, after(k, held))
        return ahead

    def local(where):
        def thunk(held):
            n = 2 * groups.index(where)
            args = after((queries, k, v, gate_rows, cotangent), held)
            return run(
                functools.partial(local_kernel, plan, where),
                [plan.low, plan.full, plan.low, plan.square, plan.full, plan.full],
                *args,
                *ahead[n : n + 2],
            )

        return thunk

    thunks = [local(where) for where in groups]
    pieces, made = carried(plan, sums, early, ([], thunks, []), False)
    made = dict(zip(groups, made))
    lk, slope, lq, weights, inside, gated = ({w: made[w][n] for w in groups} for n in range(6))
    state, attended, running = {}, {}, ()
    for n, where in enumerate(late):
        last = n == count - 1
        state[where], attended[where], *running = run(
            functools.partial(attend_kernel, plan, where[1], n == 0, last),
            [plan.state, plan.full] + ([plan.sums] if last else [plan.wide] * 2),
            *pieces[where],
            lq[where],
            inside[where],
            gated[where],
            *running,
        )
    scales = head_total(running[0])
    d_attn, sums = {}, {}
    for n, where in enumerate(groups):
        total = plan.block if n == 0 and plan.split else plan.tall
        d_attn[where], sums[where], *more = run(
            functools.partial(grad_kernel, plan, n == 0),
            [plan.low, total] + ([plan.wide] * 2 if n == 0 else []),
            *scales,
            attended[where],
            gated[where],
            lq[where],
        )
        scales = more or scales
        if n == 0:
            sums[where] = [sums[where]]
            if plan.split:
                second = functools.partial(section_kernel, plan, 1)
                sums[where].append(run(second, plan.block, lq[where], d_attn[where]))
    gates = []

    def early_gates(held):
        args = (scales[0], gate_rows, *(attended[w] for w in groups), *(gated[w] for w in groups))
        kernel = functools.partial(early_gate_kernel, plan, groups)
        gates[:] = run(kernel, [plan.low] * count, *after(args, held))
        return gates

    outer = []

    def inner(where):
        def thunk(held):
            first = not outer
            args = after(
                (
                    state[where], scales[0], weights[where], d_attn[where], lq[where], lk[where],
                    attended[where], gated[where], queries, v, gate_rows,
                    gates[groups.index(where)],
                ),
                held,
            )
            gq, gg, pk, pv = run(
                functools.partial(inside_kernel, plan, where, first),
                [plan.given, plan.given, plan.full, plan.full],
                *args,
                *outer,
                scratch=[pltpu.VMEM((plan.rows, plan.span), BF16)] * 2
                + [pltpu.SemaphoreType.DMA((2,))],
                in_specs=[VMEM] * 12 + [ANY] * len(outer),
                out_specs=[ANY, ANY, VMEM, VMEM],
                aliases={} if first else {12: 0, 13: 1},
            )
            outer[:] = [gq, gg]
            return pk, pv

        return thunk

    thunks = [inner(where) for where in groups]
    pieces, made = carried(plan, sums, early_gates, (thunks[:1], thunks[1:], []), True)
    made = dict(zip(groups, made))
    where = (0, 1)
    state_scratch = pltpu.VMEM((plan.span, DH), BF16)
    ends = run(
        functools.partial(finish_kernel, plan, where),
        [plan.low, plan.low],
        *pieces[where],
        slope[where],
        v,
        lk[where],
        *made[where],
        scratch=[state_scratch],
    )
    where = (0, 0)
    ends = run(
        functools.partial(finish_kernel, plan, where),
        [plan.given, plan.given],
        *pieces[where],
        slope[where],
        v,
        lk[where],
        *made[where],
        *ends,
        scratch=[state_scratch]
        + [pltpu.VMEM((plan.rows, plan.span), BF16)] * 2
        + [pltpu.SemaphoreType.DMA((2 + 2 * plan.group // plan.batch,))],
        in_specs=[VMEM] * 11,
        out_specs=[ANY, ANY],
    )
    return (outer[0], ends[0], ends[1], outer[1])


def solution(mesh):
    spec = P("ctx", "head")
    return jax.shard_map(
        per_device, mesh=mesh, in_specs=(spec,) * 5, out_specs=(spec,) * 4, check_vma=False
    )
```

```python
import functools

import jax
import jax.numpy as jnp
from jax import lax
from jax.experimental import pallas as pl
from jax.experimental.pallas import tpu as pltpu
from jax.sharding import PartitionSpec as P

H = 32
DH = 128
EPSILON = 1e-06
QUAD = 4
SECTIONS = ((1, 2), (3, 0))
GATHER = ((0, 1, 2, 3), (0, 1, 2, 3))
HAND = ((0, 1, 2, 3), (0, 3, 1, 2))
CHUNKS = 1
BATCH = 4
F32 = jnp.float32
BF16 = jnp.bfloat16
SMALL = 16 * 1024 * 1024
LARGE = 60 * 1024 * 1024
ANY = pl.BlockSpec(memory_space=pl.ANY)
VMEM = pl.BlockSpec(memory_space=pltpu.VMEM)


def dot(a, b, ca, cb):
    return lax.dot_general(a, b, (((ca,), (cb,)), ((), ())), preferred_element_type=F32)


def sigmoid(x):
    return 0.5 + 0.5 * jnp.tanh(0.5 * x)


def thirds(x):
    first = x.astype(BF16)
    rest = x - first.astype(F32)
    second = rest.astype(BF16)
    return [first, second, (rest - second.astype(F32)).astype(BF16)]


def chooser(rows, width):
    line = lax.broadcasted_iota(jnp.int32, (rows, width), 0)
    column = lax.broadcasted_iota(jnp.int32, (rows, width), 1)
    return jnp.where(line == column // DH, 1.0, 0.0).astype(BF16)


def core_of():
    return lax.rem(lax.axis_index("ctx"), 2)


def chip_of():
    return lax.rem(lax.axis_index("ctx") // 2, QUAD)


def mate(orders, n, other=0):
    first, second = orders[0][n], orders[1][n]
    return first + (core_of() ^ other) * (second - first)


def head(g):
    return slice(g * DH, (g + 1) * DH)


def after(values, done):
    flat, tree = jax.tree.flatten(values)
    out = lax.optimization_barrier(tuple(flat) + tuple(jax.tree.leaves(done)))
    return jax.tree.unflatten(tree, out[: len(flat)])


class Plan:
    def __init__(self, rows, width):
        self.rows, self.width = rows, width
        self.heads = width // DH
        self.group = self.heads // (2 * CHUNKS)
        self.span = self.group * DH
        self.batch = BATCH if self.group % BATCH == 0 else 1
        self.part = self.span // QUAD
        self.split = self.part % DH == 0
        self.block = jax.ShapeDtypeStruct((2 * self.part, DH), F32)
        self.tall = jax.ShapeDtypeStruct((self.span, DH), F32)
        self.piece = jax.ShapeDtypeStruct((self.part, DH), F32)
        self.low = jax.ShapeDtypeStruct((rows, self.span), BF16)
        self.full = jax.ShapeDtypeStruct((rows, self.span), F32)
        self.wide = jax.ShapeDtypeStruct((rows, DH), F32)
        self.square = jax.ShapeDtypeStruct((self.group, rows, rows), BF16)
        self.state = jax.ShapeDtypeStruct((self.span, DH), BF16)
        self.given = jax.ShapeDtypeStruct((rows, width), BF16)
        self.sums = jax.ShapeDtypeStruct((8, rows), F32)

    def start(self, chunk, side):
        half = lax.rem(core_of() + 1 + side, 2)
        return pl.multiple_of((half * CHUNKS + chunk) * self.span, self.span)

    def columns(self, chunk, side, g=None):
        start = self.start(chunk, side)
        if g is None:
            return pl.ds(start, self.span)
        return pl.ds(pl.multiple_of(start + g * DH, DH), DH)


    def section(self, n):
        count = self.part // DH
        chip = chip_of()
        return [(chip ^ k) * count + h for k in SECTIONS[n] for h in range(count)]

    def own_part(self, k):
        return pl.ds(pl.multiple_of((chip_of() ^ k) * self.part, self.part), self.part)


def run(kernel, out_shape, *args, scratch=(), in_specs=None, out_specs=None, limit=SMALL, aliases=None):
    extra = {}
    if in_specs is not None:
        extra["in_specs"] = in_specs
    if out_specs is not None:
        extra["out_specs"] = out_specs
    if aliases:
        extra["input_output_aliases"] = aliases
    return pl.pallas_call(
        kernel,
        out_shape=out_shape,
        scratch_shapes=list(scratch),
        compiler_params=pltpu.CompilerParams(vmem_limit_bytes=limit),
        **extra,
    )(*args)


def key_state(k, v):
    return dot((k * sigmoid(k)).astype(BF16), v, 0, 0)


def first_kernel(plan, order, k_hbm, v_hbm, k_ref, v_ref, out_ref, sems):
    copies = []
    for n, where in enumerate(order):
        at = (slice(None), plan.columns(*where))
        for m, (source, target) in enumerate(((k_hbm, k_ref), (v_hbm, v_ref))):
            copy = pltpu.make_async_copy(source.at[at], target.at[at], sems.at[2 * n + m])
            copy.start()
            copies.append(copy)
    copies[0].wait()
    copies[1].wait()
    next_kernel(plan, order[0], 0 if plan.split else None, k_ref, v_ref, out_ref)
    for copy in copies[2:]:
        copy.wait()


def next_kernel(plan, where, section, k_ref, v_ref, out_ref):
    heads = range(plan.group) if section is None else plan.section(section)
    for n, g in enumerate(heads):
        at = plan.columns(*where, g)
        out_ref[head(n), :] = key_state(k_ref[:, at].astype(F32), v_ref[:, at])


def causal_mask(rows):
    return lax.broadcasted_iota(jnp.int32, (rows, rows), 0) >= lax.broadcasted_iota(
        jnp.int32, (rows, rows), 1
    )


def key_part(plan, where, k_ref, lk_ref, slope_ref):
    for g in range(plan.group):
        k = k_ref[:, plan.columns(*where, g)].astype(F32)
        sig = sigmoid(k)
        lk_ref[:, head(g)] = (k * sig).astype(BF16)
        slope_ref[:, head(g)] = sig * (1.0 + k * (1.0 - sig))


def early_key_kernel(plan, groups, k_ref, *outs):
    @pl.when(core_of() == 0)
    def _():
        for n, where in enumerate(groups):
            key_part(plan, where, k_ref, *outs[2 * n : 2 * n + 2])


def local_kernel(plan, where, q_ref, k_ref, v_ref, gate_ref, cot_ref, *refs):
    early, keys, (lq_ref, w_ref, att_ref, gated_ref) = refs[:2], refs[2:4], refs[4:]

    @pl.when(core_of() == 0)
    def _():
        for made, out in zip(early, keys):
            out[...] = made[...]

    @pl.when(core_of() == 1)
    def _():
        key_part(plan, where, k_ref, *keys)

    causal = causal_mask(plan.rows)
    for g in range(plan.group):
        at = plan.columns(*where, g)
        q = q_ref[:, at].astype(F32)
        lq = (q * sigmoid(q)).astype(BF16)
        lq_ref[:, head(g)] = lq
        weights = jnp.where(causal, dot(lq, keys[0][:, head(g)], 1, 1), 0.0).astype(BF16)
        w_ref[g] = weights
        att_ref[:, head(g)] = dot(weights, v_ref[:, at], 1, 0)
        gated_ref[:, head(g)] = cot_ref[:, at].astype(F32) * sigmoid(gate_ref[:, at].astype(F32))


def gate_part(plan, where, inv_ref, gate_ref, att_ref, gated_ref, out_ref):
    for g in range(plan.group):
        gate = sigmoid(gate_ref[:, plan.columns(*where, g)].astype(F32))
        normed = att_ref[:, head(g)] * inv_ref[...]
        out_ref[:, head(g)] = (gated_ref[:, head(g)] * normed * (1.0 - gate)).astype(BF16)


def early_gate_kernel(plan, groups, inv_ref, gate_ref, *refs):
    count = len(groups)

    @pl.when(core_of() == 0)
    def _():
        for n, where in enumerate(groups):
            att_ref, gated_ref, out_ref = refs[n::count]
            gate_part(plan, where, inv_ref, gate_ref, att_ref, gated_ref, out_ref)


def place_state(plan, reverse, side, pieces, add_ref, state_ref):
    add = core_of() == (0 if reverse else 1)
    for slot in range(QUAD):
        k = mate(HAND, slot, 1 - side)
        piece = pieces[slot][...]
        if add_ref:
            piece = piece + jnp.where(add, near_part(plan, add_ref, k), 0.0)
        state_ref[plan.own_part(k), :] = piece.astype(BF16)


def near_part(plan, refs, k):
    if len(refs) == 1:
        return refs[0][plan.own_part(k), :]
    place = lax.rem(k + QUAD - 1, QUAD)
    here = pl.ds(pl.multiple_of(lax.rem(place, 2) * plan.part, plan.part), plan.part)
    return jnp.where(place < 2, refs[0][here, :], refs[1][here, :])


def attend_kernel(plan, side, first, last, *refs):
    extra = side * (1 + plan.split)
    pieces, add_ref = refs[:4], refs[4 : 4 + extra]
    refs = refs[4 + extra :]
    lq_ref, local_ref, gated_ref = refs[:3]
    refs = refs[3:]
    if not first:
        square, inner = refs[0][...], refs[1][...]
        refs = refs[2:]
    state_ref, att_ref = refs[:2]
    place_state(plan, False, side, pieces, add_ref, state_ref)
    for g in range(plan.group):
        att = local_ref[:, head(g)] + dot(lq_ref[:, head(g)], state_ref[head(g), :], 1, 0)
        att_ref[:, head(g)] = att
        if first and g == 0:
            square, inner = att * att, gated_ref[:, head(g)] * att
        else:
            square, inner = square + att * att, inner + gated_ref[:, head(g)] * att
    if last:
        pick = chooser(8, 2 * DH)
        terms = thirds(jnp.concatenate([square, inner], axis=1))
        refs[2][...] = sum(dot(pick, term, 1, 1) for term in terms)
    else:
        refs[2][...] = square
        refs[3][...] = inner


def section_kernel(plan, n, lq_ref, d_ref, sum_ref):
    for place, g in enumerate(plan.section(n)):
        at = pl.ds(pl.multiple_of(g * DH, DH), DH)
        sum_ref[head(place), :] = dot(lq_ref[:, at], d_ref[:, at], 0, 0)


def grad_kernel(plan, first, a_ref, b_ref, att_ref, gated_ref, lq_ref, d_ref, sum_ref, *more):
    if first:
        total = a_ref[...] + b_ref[...]
        sumsq, raw = total[0:1, :], total[1:2, :]
        inv = 1.0 / jnp.sqrt(sumsq * (1.0 / (H * DH)) + EPSILON)
        coef = raw * inv * (1.0 / (H * DH)) * inv * inv
        line = lax.broadcasted_iota(jnp.int32, total.shape, 0)
        packed = jnp.zeros_like(total)
        for n, pair in enumerate(zip(thirds(inv), thirds(coef))):
            for m, term in enumerate(pair):
                packed = jnp.where(line == 2 * n + m, term.astype(F32), packed)
        shape = (8, 2 * DH)
        parity = lax.rem(lax.broadcasted_iota(jnp.int32, shape, 0), 2)
        side = lax.broadcasted_iota(jnp.int32, shape, 1) // DH
        pick = jnp.where(parity == side, 1.0, 0.0).astype(BF16)
        both = dot(packed.astype(BF16), pick, 0, 0)
        inv, coef = both[:, :DH], both[:, DH:]
        more[0][...] = inv
        more[1][...] = coef
    else:
        inv, coef = a_ref[...], b_ref[...]
    for g in range(plan.group):
        d = (gated_ref[:, head(g)] * inv - att_ref[:, head(g)] * coef).astype(BF16)
        d_ref[:, head(g)] = d
        if not (first and plan.split):
            sum_ref[head(g), :] = dot(lq_ref[:, head(g)], d, 0, 0)
    if first and plan.split:
        section_kernel(plan, 0, lq_ref, d_ref, sum_ref)


def inside_kernel(plan, where, first, *refs):
    (state_ref, inv_ref, w_ref, d_ref, lq_ref, lk_ref, att_ref, gated_ref) = refs[:8]
    q_ref, v_ref, gate_ref, early_ref = refs[8:12]
    gq_hbm, gg_hbm, pk_ref, pv_ref, gq, gg, sems = refs[12 if first else 14 :]

    @pl.when(core_of() == 0)
    def _():
        gg[...] = early_ref[...]

    @pl.when(core_of() == 1)
    def _():
        gate_part(plan, where, inv_ref, gate_ref, att_ref, gated_ref, gg)

    causal = causal_mask(plan.rows)
    for g in range(plan.group):
        at = plan.columns(*where, g)
        d = d_ref[:, head(g)]
        dw = jnp.where(causal, dot(d, v_ref[:, at], 1, 1), 0.0).astype(BF16)
        glq = dot(dw, lk_ref[:, head(g)], 1, 0) + dot(d, state_ref[head(g), :], 1, 1)
        q = q_ref[:, at].astype(F32)
        sig = sigmoid(q)
        gq[:, head(g)] = (glq * (sig * (1.0 + q * (1.0 - sig)))).astype(BF16)
        pk_ref[:, head(g)] = dot(dw, lq_ref[:, head(g)], 0, 0)
        pv_ref[:, head(g)] = dot(w_ref[g], d, 0, 0)
    send_out(plan, where, ((gq, gq_hbm), (gg, gg_hbm)), sems)


def send_out(plan, where, pairs, sems):
    at = (slice(None), plan.columns(*where))
    copies = [
        pltpu.make_async_copy(source, target.at[at], sems.at[n])
        for n, (source, target) in enumerate(pairs)
    ]
    for copy in copies:
        copy.start()
    for copy in copies:
        copy.wait()


def finish_kernel(plan, where, *refs):
    side = where[1]
    extra = side * (1 + plan.split)
    pieces, add_ref = refs[:4], refs[4 : 4 + extra]
    refs = refs[4 + extra :]
    slope_ref, v_ref, lk_ref, pk_ref, pv_ref = refs[:5]
    if side:
        gk, gv, state_ref = refs[5:]
    else:
        gk_done, gv_done, gk_hbm, gv_hbm, state_ref, gk, gv, sems = refs[5:]
    copies = []

    def send(pairs, at):
        for source, target in pairs:
            copy = pltpu.make_async_copy(source, target.at[:, at], sems.at[len(copies)])
            copy.start()
            copies.append(copy)

    if not side:
        send(((gk_done, gk_hbm), (gv_done, gv_hbm)), plan.columns(where[0], 1))
    place_state(plan, True, side, pieces, add_ref, state_ref)
    for g in range(plan.group):
        at = plan.columns(*where, g)
        state = state_ref[head(g), :]
        gv[:, head(g)] = (pv_ref[:, head(g)] + dot(lk_ref[:, head(g)], state, 1, 0)).astype(BF16)
        glk = pk_ref[:, head(g)] + dot(v_ref[:, at], state, 1, 1)
        gk[:, head(g)] = (glk * slope_ref[:, head(g)]).astype(BF16)
        if not side and (g + 1) % plan.batch == 0:
            first = g + 1 - plan.batch
            here = slice(first * DH, (g + 1) * DH)
            start = pl.multiple_of(plan.start(*where) + first * DH, DH)
            pairs = ((gk.at[:, here], gk_hbm), (gv.at[:, here], gv_hbm))
            send(pairs, pl.ds(start, plan.batch * DH))
    for copy in copies:
        copy.wait()


def split_kernel(plan, slots, keep_ref, got_ref, *outs):
    for n, slot in enumerate(slots):
        k = mate(GATHER, slot)
        if len(slots) == QUAD:
            here = plan.own_part(k)
        else:
            here = pl.ds(pl.multiple_of(lax.rem(k + 1, 2) * plan.part, plan.part), plan.part)
        outs[n][...] = keep_ref[plan.own_part(k), :] + got_ref[here, :]


def onward_kernel(plan, reverse, k, piece_ref, keep_ref, out_ref):
    add = core_of() == (1 if reverse else 0)
    out_ref[...] = piece_ref[...] + jnp.where(add, keep_ref[plan.own_part(mate(HAND, k)), :], 0.0)


def before_kernel(reverse, span, *refs):
    parts, got_ref, base, outs = refs[:4], refs[4], refs[5:-4], refs[-4:]
    chip = chip_of()
    far = lax.rem(lax.axis_index("ctx") // span, 2) == (0 if reverse else 1)
    start = jnp.where(far, got_ref[...], 0.0)
    for more in base:
        start = start + more[...]
    for k in range(QUAD):
        total = start
        for m in range(QUAD):
            here, there = chip ^ mate(GATHER, m), chip ^ mate(HAND, k)
            first = here > there if reverse else here < there
            total = total + jnp.where(first, parts[m][...], 0.0)
        outs[k][...] = total


def swap(x, distance):
    count = lax.axis_size("ctx")
    return lax.ppermute(x, "ctx", [(i, i ^ distance) for i in range(count)])


def quad_swap(x, slot, orders):
    count = lax.axis_size("ctx")
    return lax.ppermute(x, "ctx", [(i, i ^ 2 * orders[i % 2][slot]) for i in range(count)])


def gather_sums(plan, keep, near, early):
    first = after(near[0], early(near[0]))
    mine, came = {}, {}
    for slots, got in zip(SECTIONS if plan.split else [range(QUAD)], [first] + near[1:]):
        keep, got = after((keep, got), mine)
        made = run(
            functools.partial(split_kernel, plan, slots), [plan.piece] * len(slots), keep, got
        )
        for slot, x in zip(slots, made):
            mine[slot] = x
            if slot:
                came[slot] = quad_swap(x, slot, GATHER)
    return [mine[0]], [came[slot] for slot in range(1, QUAD)]


def across(parts, reverse):
    count = lax.axis_size("ctx")
    total = (parts[0] + parts[1]) + (parts[2] + parts[3])
    held = total
    base = []
    span = 2 * QUAD
    while True:
        got = swap(total, span)
        if 2 * span >= count:
            return held, (got, base, span)
        far = lax.rem(lax.axis_index("ctx") // span, 2) == (0 if reverse else 1)
        term = jnp.where(far, got, 0.0)
        base = [base[0] + term] if base else [term]
        total = total + got
        span *= 2


def hand_out(plan, parts, got, base, span, reverse):
    outs = run(
        functools.partial(before_kernel, reverse, span),
        [plan.piece] * QUAD,
        *parts,
        got,
        *base,
    )
    return outs, [quad_swap(outs[k], k, HAND) for k in range(1, QUAD)]


def carried(plan, sums_of, early, work, reverse):
    near = [swap(x, 1) for x in sums_of[0, 0]]
    keep = sums_of[0, 1]
    own, came = gather_sums(plan, keep, near, early)
    results = []

    def meanwhile(thunks, held, values):
        done = [t(held) for t in thunks]
        results.extend(done)
        return after(values, done) if done else values

    parts = own + meanwhile(work[0], own[0], came)
    held, (got, base, span) = across(parts, reverse)
    got = meanwhile(work[1], held, got)
    outs, came = hand_out(plan, parts, got, base, span, reverse)
    came = meanwhile(work[2], outs[0], came)
    own = [outs[0]] + came
    pieces = {(0, 1): own + near}
    pieces[0, 0] = [
        swap(run(functools.partial(onward_kernel, plan, reverse, k), plan.piece, x, keep), 1)
        for k, x in enumerate(own)
    ]
    return pieces, results


def head_total(sums):
    if lax.axis_size("head") == 2:
        return sums, lax.ppermute(sums, "head", [(0, 1), (1, 0)])
    return lax.psum(sums, "head"), jnp.zeros_like(sums)


def per_device(queries, key_rows, value_rows, gate_rows, cotangent):
    plan = Plan(*queries.shape)
    groups = [(c, side) for c in range(CHUNKS) for side in (0, 1)]
    late = [(c, side) for c in range(CHUNKS) for side in (1, 0)]
    count = len(groups)
    k, v, first_sum = run(
        functools.partial(first_kernel, plan, groups),
        [plan.given, plan.given, plan.block if plan.split else plan.tall],
        pltpu.with_memory_space_constraint(key_rows, pltpu.HBM),
        pltpu.with_memory_space_constraint(value_rows, pltpu.HBM),
        scratch=[pltpu.SemaphoreType.DMA((2 * count,))],
        in_specs=[ANY, ANY],
    )
    sums = {groups[0]: [first_sum]}
    if plan.split:
        second = functools.partial(next_kernel, plan, groups[0], 1)
        sums[groups[0]].append(run(second, plan.block, k, v))
    sums[groups[1]] = run(functools.partial(next_kernel, plan, groups[1], None), plan.tall, k, v)

    ahead = []

    def early(held):
        kernel = functools.partial(early_key_kernel, plan, groups)
        ahead[:] = run(kernel, [plan.low, plan.full] * count, after(k, held))
        return ahead

    def local(where):
        def thunk(held):
            n = 2 * groups.index(where)
            args = after((queries, k, v, gate_rows, cotangent), held)
            return run(
                functools.partial(local_kernel, plan, where),
                [plan.low, plan.full, plan.low, plan.square, plan.full, plan.full],
                *args,
                *ahead[n : n + 2],
            )

        return thunk

    thunks = [local(where) for where in groups]
    pieces, made = carried(plan, sums, early, ([], thunks, []), False)
    made = dict(zip(groups, made))
    lk, slope, lq, weights, inside, gated = ({w: made[w][n] for w in groups} for n in range(6))
    state, attended, running = {}, {}, ()
    for n, where in enumerate(late):
        last = n == count - 1
        state[where], attended[where], *running = run(
            functools.partial(attend_kernel, plan, where[1], n == 0, last),
            [plan.state, plan.full] + ([plan.sums] if last else [plan.wide] * 2),
            *pieces[where],
            lq[where],
            inside[where],
            gated[where],
            *running,
        )
    scales = head_total(running[0])
    d_attn, sums = {}, {}
    for n, where in enumerate(groups):
        total = plan.block if n == 0 and plan.split else plan.tall
        d_attn[where], sums[where], *more = run(
            functools.partial(grad_kernel, plan, n == 0),
            [plan.low, total] + ([plan.wide] * 2 if n == 0 else []),
            *scales,
            attended[where],
            gated[where],
            lq[where],
        )
        scales = more or scales
        if n == 0:
            sums[where] = [sums[where]]
            if plan.split:
                second = functools.partial(section_kernel, plan, 1)
                sums[where].append(run(second, plan.block, lq[where], d_attn[where]))
    gates = []

    def early_gates(held):
        args = (scales[0], gate_rows, *(attended[w] for w in groups), *(gated[w] for w in groups))
        kernel = functools.partial(early_gate_kernel, plan, groups)
        gates[:] = run(kernel, [plan.low] * count, *after(args, held))
        return gates

    outer = []

    def inner(where):
        def thunk(held):
            first = not outer
            args = after(
                (
                    state[where], scales[0], weights[where], d_attn[where], lq[where], lk[where],
                    attended[where], gated[where], queries, v, gate_rows,
                    gates[groups.index(where)],
                ),
                held,
            )
            gq, gg, pk, pv = run(
                functools.partial(inside_kernel, plan, where, first),
                [plan.given, plan.given, plan.full, plan.full],
                *args,
                *outer,
                scratch=[pltpu.VMEM((plan.rows, plan.span), BF16)] * 2
                + [pltpu.SemaphoreType.DMA((2,))],
                in_specs=[VMEM] * 12 + [ANY] * len(outer),
                out_specs=[ANY, ANY, VMEM, VMEM],
                aliases={} if first else {12: 0, 13: 1},
            )
            outer[:] = [gq, gg]
            return pk, pv

        return thunk

    thunks = [inner(where) for where in groups]
    pieces, made = carried(plan, sums, early_gates, (thunks[:1], thunks[1:], []), True)
    made = dict(zip(groups, made))
    where = (0, 1)
    state_scratch = pltpu.VMEM((plan.span, DH), BF16)
    ends = run(
        functools.partial(finish_kernel, plan, where),
        [plan.low, plan.low],
        *pieces[where],
        slope[where],
        v,
        lk[where],
        *made[where],
        scratch=[state_scratch],
    )
    where = (0, 0)
    ends = run(
        functools.partial(finish_kernel, plan, where),
        [plan.given, plan.given],
        *pieces[where],
        slope[where],
        v,
        lk[where],
        *made[where],
        *ends,
        scratch=[state_scratch]
        + [pltpu.VMEM((plan.rows, plan.span), BF16)] * 2
        + [pltpu.SemaphoreType.DMA((2 + 2 * plan.group // plan.batch,))],
        in_specs=[VMEM] * 11,
        out_specs=[ANY, ANY],
    )
    return (outer[0], ends[0], ends[1], outer[1])


def solution(mesh):
    spec = P("ctx", "head")
    return jax.shard_map(
        per_device, mesh=mesh, in_specs=(spec,) * 5, out_specs=(spec,) * 4, check_vma=False
    )
```

```python
import functools

import jax
import jax.numpy as jnp
from jax import lax
from jax.experimental import pallas as pl
from jax.experimental.pallas import tpu as pltpu
from jax.sharding import PartitionSpec as P

H = 32
DH = 128
EPSILON = 1e-06
QUAD = 4
SECTIONS = ((1, 2), (3, 0))
GATHER = ((0, 1, 2, 3), (0, 1, 2, 3))
HAND = ((0, 1, 2, 3), (0, 3, 1, 2))
CHUNKS = 1
BATCH = 4
F32 = jnp.float32
BF16 = jnp.bfloat16
SMALL = 16 * 1024 * 1024
LARGE = 60 * 1024 * 1024
ANY = pl.BlockSpec(memory_space=pl.ANY)
VMEM = pl.BlockSpec(memory_space=pltpu.VMEM)


def dot(a, b, ca, cb):
    return lax.dot_general(a, b, (((ca,), (cb,)), ((), ())), preferred_element_type=F32)


def sigmoid(x):
    return 0.5 + 0.5 * jnp.tanh(0.5 * x)


def thirds(x):
    first = x.astype(BF16)
    rest = x - first.astype(F32)
    second = rest.astype(BF16)
    return [first, second, (rest - second.astype(F32)).astype(BF16)]


def chooser(rows, width):
    line = lax.broadcasted_iota(jnp.int32, (rows, width), 0)
    column = lax.broadcasted_iota(jnp.int32, (rows, width), 1)
    return jnp.where(line == column // DH, 1.0, 0.0).astype(BF16)


def core_of():
    return lax.rem(lax.axis_index("ctx"), 2)


def chip_of():
    return lax.rem(lax.axis_index("ctx") // 2, QUAD)


def mate(orders, n, other=0):
    first, second = orders[0][n], orders[1][n]
    return first + (core_of() ^ other) * (second - first)


def head(g):
    return slice(g * DH, (g + 1) * DH)


def after(values, done):
    flat, tree = jax.tree.flatten(values)
    out = lax.optimization_barrier(tuple(flat) + tuple(jax.tree.leaves(done)))
    return jax.tree.unflatten(tree, out[: len(flat)])


class Plan:
    def __init__(self, rows, width):
        self.rows, self.width = rows, width
        self.heads = width // DH
        self.group = self.heads // (2 * CHUNKS)
        self.span = self.group * DH
        self.batch = BATCH if self.group % BATCH == 0 else 1
        self.part = self.span // QUAD
        self.split = self.part % DH == 0
        self.block = jax.ShapeDtypeStruct((2 * self.part, DH), F32)
        self.tall = jax.ShapeDtypeStruct((self.span, DH), F32)
        self.piece = jax.ShapeDtypeStruct((self.part, DH), F32)
        self.low = jax.ShapeDtypeStruct((rows, self.span), BF16)
        self.full = jax.ShapeDtypeStruct((rows, self.span), F32)
        self.wide = jax.ShapeDtypeStruct((rows, DH), F32)
        self.square = jax.ShapeDtypeStruct((self.group, rows, rows), BF16)
        self.state = jax.ShapeDtypeStruct((self.span, DH), BF16)
        self.given = jax.ShapeDtypeStruct((rows, width), BF16)
        self.sums = jax.ShapeDtypeStruct((8, rows), F32)

    def start(self, chunk, side):
        half = lax.rem(core_of() + 1 + side, 2)
        return pl.multiple_of((half * CHUNKS + chunk) * self.span, self.span)

    def columns(self, chunk, side, g=None):
        start = self.start(chunk, side)
        if g is None:
            return pl.ds(start, self.span)
        return pl.ds(pl.multiple_of(start + g * DH, DH), DH)


    def section(self, n):
        count = self.part // DH
        chip = chip_of()
        return [(chip ^ k) * count + h for k in SECTIONS[n] for h in range(count)]

    def own_part(self, k):
        return pl.ds(pl.multiple_of((chip_of() ^ k) * self.part, self.part), self.part)


def run(kernel, out_shape, *args, scratch=(), in_specs=None, out_specs=None, limit=SMALL, aliases=None):
    extra = {}
    if in_specs is not None:
        extra["in_specs"] = in_specs
    if out_specs is not None:
        extra["out_specs"] = out_specs
    if aliases:
        extra["input_output_aliases"] = aliases
    return pl.pallas_call(
        kernel,
        out_shape=out_shape,
        scratch_shapes=list(scratch),
        compiler_params=pltpu.CompilerParams(vmem_limit_bytes=limit),
        **extra,
    )(*args)


def key_state(k, v):
    return dot((k * sigmoid(k)).astype(BF16), v, 0, 0)


def first_kernel(plan, order, k_hbm, v_hbm, k_ref, v_ref, out_ref, sems):
    copies = []
    for n, where in enumerate(order):
        at = (slice(None), plan.columns(*where))
        for m, (source, target) in enumerate(((k_hbm, k_ref), (v_hbm, v_ref))):
            copy = pltpu.make_async_copy(source.at[at], target.at[at], sems.at[2 * n + m])
            copy.start()
            copies.append(copy)
    copies[0].wait()
    copies[1].wait()
    next_kernel(plan, order[0], 0 if plan.split else None, k_ref, v_ref, out_ref)
    for copy in copies[2:]:
        copy.wait()


def next_kernel(plan, where, section, k_ref, v_ref, out_ref):
    heads = range(plan.group) if section is None else plan.section(section)
    for n, g in enumerate(heads):
        at = plan.columns(*where, g)
        out_ref[head(n), :] = key_state(k_ref[:, at].astype(F32), v_ref[:, at])


def causal_mask(rows):
    return lax.broadcasted_iota(jnp.int32, (rows, rows), 0) >= lax.broadcasted_iota(
        jnp.int32, (rows, rows), 1
    )


def key_part(plan, where, k_ref, lk_ref, slope_ref):
    for g in range(plan.group):
        k = k_ref[:, plan.columns(*where, g)].astype(F32)
        sig = sigmoid(k)
        lk_ref[:, head(g)] = (k * sig).astype(BF16)
        slope_ref[:, head(g)] = sig * (1.0 + k * (1.0 - sig))


def early_key_kernel(plan, groups, k_ref, *outs):
    @pl.when(core_of() == 0)
    def _():
        for n, where in enumerate(groups):
            key_part(plan, where, k_ref, *outs[2 * n : 2 * n + 2])


def local_kernel(plan, where, q_ref, k_ref, v_ref, gate_ref, cot_ref, *refs):
    early, keys, (lq_ref, w_ref, att_ref, gated_ref) = refs[:2], refs[2:4], refs[4:]

    @pl.when(core_of() == 0)
    def _():
        for made, out in zip(early, keys):
            out[...] = made[...]

    @pl.when(core_of() == 1)
    def _():
        key_part(plan, where, k_ref, *keys)

    causal = causal_mask(plan.rows)
    for g in range(plan.group):
        at = plan.columns(*where, g)
        q = q_ref[:, at].astype(F32)
        lq = (q * sigmoid(q)).astype(BF16)
        lq_ref[:, head(g)] = lq
        weights = jnp.where(causal, dot(lq, keys[0][:, head(g)], 1, 1), 0.0).astype(BF16)
        w_ref[g] = weights
        att_ref[:, head(g)] = dot(weights, v_ref[:, at], 1, 0)
        gated_ref[:, head(g)] = cot_ref[:, at].astype(F32) * sigmoid(gate_ref[:, at].astype(F32))


def gate_part(plan, where, inv_ref, gate_ref, att_ref, gated_ref, out_ref):
    for g in range(plan.group):
        gate = sigmoid(gate_ref[:, plan.columns(*where, g)].astype(F32))
        normed = att_ref[:, head(g)] * inv_ref[...]
        out_ref[:, head(g)] = (gated_ref[:, head(g)] * normed * (1.0 - gate)).astype(BF16)


def early_gate_kernel(plan, groups, inv_ref, gate_ref, *refs):
    count = len(groups)

    @pl.when(core_of() == 0)
    def _():
        for n, where in enumerate(groups):
            att_ref, gated_ref, out_ref = refs[n::count]
            gate_part(plan, where, inv_ref, gate_ref, att_ref, gated_ref, out_ref)


def place_state(plan, reverse, side, pieces, add_ref, state_ref):
    add = core_of() == (0 if reverse else 1)
    for slot in range(QUAD):
        k = mate(HAND, slot, 1 - side)
        piece = pieces[slot][...]
        if add_ref:
            piece = piece + jnp.where(add, near_part(plan, add_ref, k), 0.0)
        state_ref[plan.own_part(k), :] = piece.astype(BF16)


def near_part(plan, refs, k):
    if len(refs) == 1:
        return refs[0][plan.own_part(k), :]
    place = lax.rem(k + QUAD - 1, QUAD)
    here = pl.ds(pl.multiple_of(lax.rem(place, 2) * plan.part, plan.part), plan.part)
    return jnp.where(place < 2, refs[0][here, :], refs[1][here, :])


def attend_kernel(plan, side, first, last, *refs):
    extra = side * (1 + plan.split)
    pieces, add_ref = refs[:4], refs[4 : 4 + extra]
    refs = refs[4 + extra :]
    lq_ref, local_ref, gated_ref = refs[:3]
    refs = refs[3:]
    if not first:
        square, inner = refs[0][...], refs[1][...]
        refs = refs[2:]
    state_ref, att_ref = refs[:2]
    place_state(plan, False, side, pieces, add_ref, state_ref)
    for g in range(plan.group):
        att = local_ref[:, head(g)] + dot(lq_ref[:, head(g)], state_ref[head(g), :], 1, 0)
        att_ref[:, head(g)] = att
        if first and g == 0:
            square, inner = att * att, gated_ref[:, head(g)] * att
        else:
            square, inner = square + att * att, inner + gated_ref[:, head(g)] * att
    if last:
        pick = jnp.concatenate([chooser(8, 2 * DH)] * 3, axis=1)
        terms = thirds(jnp.concatenate([square, inner], axis=1))
        refs[2][...] = dot(pick, jnp.concatenate(terms, axis=1), 1, 1)
    else:
        refs[2][...] = square
        refs[3][...] = inner


def section_kernel(plan, n, lq_ref, d_ref, sum_ref):
    for place, g in enumerate(plan.section(n)):
        at = pl.ds(pl.multiple_of(g * DH, DH), DH)
        sum_ref[head(place), :] = dot(lq_ref[:, at], d_ref[:, at], 0, 0)


def grad_kernel(plan, first, a_ref, b_ref, att_ref, gated_ref, lq_ref, d_ref, sum_ref, *more):
    if first:
        total = a_ref[...] + b_ref[...]
        sumsq, raw = total[0:1, :], total[1:2, :]
        inv = 1.0 / jnp.sqrt(sumsq * (1.0 / (H * DH)) + EPSILON)
        coef = raw * inv * (1.0 / (H * DH)) * inv * inv
        line = lax.broadcasted_iota(jnp.int32, total.shape, 0)
        packed = jnp.zeros_like(total)
        for n, pair in enumerate(zip(thirds(inv), thirds(coef))):
            for m, term in enumerate(pair):
                packed = jnp.where(line == 2 * n + m, term.astype(F32), packed)
        shape = (8, 2 * DH)
        parity = lax.rem(lax.broadcasted_iota(jnp.int32, shape, 0), 2)
        side = lax.broadcasted_iota(jnp.int32, shape, 1) // DH
        pick = jnp.where(parity == side, 1.0, 0.0).astype(BF16)
        both = dot(packed.astype(BF16), pick, 0, 0)
        inv, coef = both[:, :DH], both[:, DH:]
        more[0][...] = inv
        more[1][...] = coef
    else:
        inv, coef = a_ref[...], b_ref[...]
    for g in range(plan.group):
        d = (gated_ref[:, head(g)] * inv - att_ref[:, head(g)] * coef).astype(BF16)
        d_ref[:, head(g)] = d
        if not (first and plan.split):
            sum_ref[head(g), :] = dot(lq_ref[:, head(g)], d, 0, 0)
    if first and plan.split:
        section_kernel(plan, 0, lq_ref, d_ref, sum_ref)


def inside_kernel(plan, where, first, *refs):
    (state_ref, inv_ref, w_ref, d_ref, lq_ref, lk_ref, att_ref, gated_ref) = refs[:8]
    q_ref, v_ref, gate_ref, early_ref = refs[8:12]
    gq_hbm, gg_hbm, pk_ref, pv_ref, gq, gg, sems = refs[12 if first else 14 :]

    @pl.when(core_of() == 0)
    def _():
        gg[...] = early_ref[...]

    @pl.when(core_of() == 1)
    def _():
        gate_part(plan, where, inv_ref, gate_ref, att_ref, gated_ref, gg)

    causal = causal_mask(plan.rows)
    for g in range(plan.group):
        at = plan.columns(*where, g)
        d = d_ref[:, head(g)]
        dw = jnp.where(causal, dot(d, v_ref[:, at], 1, 1), 0.0).astype(BF16)
        glq = dot(dw, lk_ref[:, head(g)], 1, 0) + dot(d, state_ref[head(g), :], 1, 1)
        q = q_ref[:, at].astype(F32)
        sig = sigmoid(q)
        gq[:, head(g)] = (glq * (sig * (1.0 + q * (1.0 - sig)))).astype(BF16)
        pk_ref[:, head(g)] = dot(dw, lq_ref[:, head(g)], 0, 0)
        pv_ref[:, head(g)] = dot(w_ref[g], d, 0, 0)
    send_out(plan, where, ((gq, gq_hbm), (gg, gg_hbm)), sems)


def send_out(plan, where, pairs, sems):
    at = (slice(None), plan.columns(*where))
    copies = [
        pltpu.make_async_copy(source, target.at[at], sems.at[n])
        for n, (source, target) in enumerate(pairs)
    ]
    for copy in copies:
        copy.start()
    for copy in copies:
        copy.wait()


def finish_kernel(plan, where, *refs):
    side = where[1]
    extra = side * (1 + plan.split)
    pieces, add_ref = refs[:4], refs[4 : 4 + extra]
    refs = refs[4 + extra :]
    slope_ref, v_ref, lk_ref, pk_ref, pv_ref = refs[:5]
    if side:
        gk, gv, state_ref = refs[5:]
    else:
        gk_done, gv_done, gk_hbm, gv_hbm, state_ref, gk, gv, sems = refs[5:]
    copies = []

    def send(pairs, at):
        for source, target in pairs:
            copy = pltpu.make_async_copy(source, target.at[:, at], sems.at[len(copies)])
            copy.start()
            copies.append(copy)

    if not side:
        send(((gk_done, gk_hbm), (gv_done, gv_hbm)), plan.columns(where[0], 1))
    place_state(plan, True, side, pieces, add_ref, state_ref)
    for g in range(plan.group):
        at = plan.columns(*where, g)
        state = state_ref[head(g), :]
        gv[:, head(g)] = (pv_ref[:, head(g)] + dot(lk_ref[:, head(g)], state, 1, 0)).astype(BF16)
        glk = pk_ref[:, head(g)] + dot(v_ref[:, at], state, 1, 1)
        gk[:, head(g)] = (glk * slope_ref[:, head(g)]).astype(BF16)
        if not side and (g + 1) % plan.batch == 0:
            first = g + 1 - plan.batch
            here = slice(first * DH, (g + 1) * DH)
            start = pl.multiple_of(plan.start(*where) + first * DH, DH)
            pairs = ((gk.at[:, here], gk_hbm), (gv.at[:, here], gv_hbm))
            send(pairs, pl.ds(start, plan.batch * DH))
    for copy in copies:
        copy.wait()


def split_kernel(plan, slots, keep_ref, got_ref, *outs):
    for n, slot in enumerate(slots):
        k = mate(GATHER, slot)
        if len(slots) == QUAD:
            here = plan.own_part(k)
        else:
            here = pl.ds(pl.multiple_of(lax.rem(k + 1, 2) * plan.part, plan.part), plan.part)
        outs[n][...] = keep_ref[plan.own_part(k), :] + got_ref[here, :]


def onward_kernel(plan, reverse, k, piece_ref, keep_ref, out_ref):
    add = core_of() == (1 if reverse else 0)
    out_ref[...] = piece_ref[...] + jnp.where(add, keep_ref[plan.own_part(mate(HAND, k)), :], 0.0)


def before_kernel(reverse, span, *refs):
    parts, got_ref, base, outs = refs[:4], refs[4], refs[5:-4], refs[-4:]
    chip = chip_of()
    far = lax.rem(lax.axis_index("ctx") // span, 2) == (0 if reverse else 1)
    start = jnp.where(far, got_ref[...], 0.0)
    for more in base:
        start = start + more[...]
    for k in range(QUAD):
        total = start
        for m in range(QUAD):
            here, there = chip ^ mate(GATHER, m), chip ^ mate(HAND, k)
            first = here > there if reverse else here < there
            total = total + jnp.where(first, parts[m][...], 0.0)
        outs[k][...] = total


def swap(x, distance):
    count = lax.axis_size("ctx")
    return lax.ppermute(x, "ctx", [(i, i ^ distance) for i in range(count)])


def quad_swap(x, slot, orders):
    count = lax.axis_size("ctx")
    return lax.ppermute(x, "ctx", [(i, i ^ 2 * orders[i % 2][slot]) for i in range(count)])


def gather_sums(plan, keep, near, early):
    first = after(near[0], early(near[0]))
    mine, came = {}, {}
    for slots, got in zip(SECTIONS if plan.split else [range(QUAD)], [first] + near[1:]):
        keep, got = after((keep, got), mine)
        made = run(
            functools.partial(split_kernel, plan, slots), [plan.piece] * len(slots), keep, got
        )
        for slot, x in zip(slots, made):
            mine[slot] = x
            if slot:
                came[slot] = quad_swap(x, slot, GATHER)
    return [mine[0]], [came[slot] for slot in range(1, QUAD)]


def across(parts, reverse):
    count = lax.axis_size("ctx")
    total = (parts[0] + parts[1]) + (parts[2] + parts[3])
    held = total
    base = []
    span = 2 * QUAD
    while True:
        got = swap(total, span)
        if 2 * span >= count:
            return held, (got, base, span)
        far = lax.rem(lax.axis_index("ctx") // span, 2) == (0 if reverse else 1)
        term = jnp.where(far, got, 0.0)
        base = [base[0] + term] if base else [term]
        total = total + got
        span *= 2


def hand_out(plan, parts, got, base, span, reverse):
    outs = run(
        functools.partial(before_kernel, reverse, span),
        [plan.piece] * QUAD,
        *parts,
        got,
        *base,
    )
    return outs, [quad_swap(outs[k], k, HAND) for k in range(1, QUAD)]


def carried(plan, sums_of, early, work, reverse):
    near = [swap(x, 1) for x in sums_of[0, 0]]
    keep = sums_of[0, 1]
    own, came = gather_sums(plan, keep, near, early)
    results = []

    def meanwhile(thunks, held, values):
        done = [t(held) for t in thunks]
        results.extend(done)
        return after(values, done) if done else values

    parts = own + meanwhile(work[0], own[0], came)
    held, (got, base, span) = across(parts, reverse)
    got = meanwhile(work[1], held, got)
    outs, came = hand_out(plan, parts, got, base, span, reverse)
    came = meanwhile(work[2], outs[0], came)
    own = [outs[0]] + came
    pieces = {(0, 1): own + near}
    pieces[0, 0] = [
        swap(run(functools.partial(onward_kernel, plan, reverse, k), plan.piece, x, keep), 1)
        for k, x in enumerate(own)
    ]
    return pieces, results


def head_total(sums):
    if lax.axis_size("head") == 2:
        return sums, lax.ppermute(sums, "head", [(0, 1), (1, 0)])
    return lax.psum(sums, "head"), jnp.zeros_like(sums)


def per_device(queries, key_rows, value_rows, gate_rows, cotangent):
    plan = Plan(*queries.shape)
    groups = [(c, side) for c in range(CHUNKS) for side in (0, 1)]
    late = [(c, side) for c in range(CHUNKS) for side in (1, 0)]
    count = len(groups)
    k, v, first_sum = run(
        functools.partial(first_kernel, plan, groups),
        [plan.given, plan.given, plan.block if plan.split else plan.tall],
        pltpu.with_memory_space_constraint(key_rows, pltpu.HBM),
        pltpu.with_memory_space_constraint(value_rows, pltpu.HBM),
        scratch=[pltpu.SemaphoreType.DMA((2 * count,))],
        in_specs=[ANY, ANY],
    )
    sums = {groups[0]: [first_sum]}
    if plan.split:
        second = functools.partial(next_kernel, plan, groups[0], 1)
        sums[groups[0]].append(run(second, plan.block, k, v))
    sums[groups[1]] = run(functools.partial(next_kernel, plan, groups[1], None), plan.tall, k, v)

    ahead = []

    def early(held):
        kernel = functools.partial(early_key_kernel, plan, groups)
        ahead[:] = run(kernel, [plan.low, plan.full] * count, after(k, held))
        return ahead

    def local(where):
        def thunk(held):
            n = 2 * groups.index(where)
            args = after((queries, k, v, gate_rows, cotangent), held)
            return run(
                functools.partial(local_kernel, plan, where),
                [plan.low, plan.full, plan.low, plan.square, plan.full, plan.full],
                *args,
                *ahead[n : n + 2],
            )

        return thunk

    thunks = [local(where) for where in groups]
    pieces, made = carried(plan, sums, early, ([], thunks, []), False)
    made = dict(zip(groups, made))
    lk, slope, lq, weights, inside, gated = ({w: made[w][n] for w in groups} for n in range(6))
    state, attended, running = {}, {}, ()
    for n, where in enumerate(late):
        last = n == count - 1
        state[where], attended[where], *running = run(
            functools.partial(attend_kernel, plan, where[1], n == 0, last),
            [plan.state, plan.full] + ([plan.sums] if last else [plan.wide] * 2),
            *pieces[where],
            lq[where],
            inside[where],
            gated[where],
            *running,
        )
    scales = head_total(running[0])
    d_attn, sums = {}, {}
    for n, where in enumerate(groups):
        total = plan.block if n == 0 and plan.split else plan.tall
        d_attn[where], sums[where], *more = run(
            functools.partial(grad_kernel, plan, n == 0),
            [plan.low, total] + ([plan.wide] * 2 if n == 0 else []),
            *scales,
            attended[where],
            gated[where],
            lq[where],
        )
        scales = more or scales
        if n == 0:
            sums[where] = [sums[where]]
            if plan.split:
                second = functools.partial(section_kernel, plan, 1)
                sums[where].append(run(second, plan.block, lq[where], d_attn[where]))
    gates = []

    def early_gates(held):
        args = (scales[0], gate_rows, *(attended[w] for w in groups), *(gated[w] for w in groups))
        kernel = functools.partial(early_gate_kernel, plan, groups)
        gates[:] = run(kernel, [plan.low] * count, *after(args, held))
        return gates

    outer = []

    def inner(where):
        def thunk(held):
            first = not outer
            args = after(
                (
                    state[where], scales[0], weights[where], d_attn[where], lq[where], lk[where],
                    attended[where], gated[where], queries, v, gate_rows,
                    gates[groups.index(where)],
                ),
                held,
            )
            gq, gg, pk, pv = run(
                functools.partial(inside_kernel, plan, where, first),
                [plan.given, plan.given, plan.full, plan.full],
                *args,
                *outer,
                scratch=[pltpu.VMEM((plan.rows, plan.span), BF16)] * 2
                + [pltpu.SemaphoreType.DMA((2,))],
                in_specs=[VMEM] * 12 + [ANY] * len(outer),
                out_specs=[ANY, ANY, VMEM, VMEM],
                aliases={} if first else {12: 0, 13: 1},
            )
            outer[:] = [gq, gg]
            return pk, pv

        return thunk

    thunks = [inner(where) for where in groups]
    pieces, made = carried(plan, sums, early_gates, (thunks[:1], thunks[1:], []), True)
    made = dict(zip(groups, made))
    where = (0, 1)
    state_scratch = pltpu.VMEM((plan.span, DH), BF16)
    ends = run(
        functools.partial(finish_kernel, plan, where),
        [plan.low, plan.low],
        *pieces[where],
        slope[where],
        v,
        lk[where],
        *made[where],
        scratch=[state_scratch],
    )
    where = (0, 0)
    ends = run(
        functools.partial(finish_kernel, plan, where),
        [plan.given, plan.given],
        *pieces[where],
        slope[where],
        v,
        lk[where],
        *made[where],
        *ends,
        scratch=[state_scratch]
        + [pltpu.VMEM((plan.rows, plan.span), BF16)] * 2
        + [pltpu.SemaphoreType.DMA((2 + 2 * plan.group // plan.batch,))],
        in_specs=[VMEM] * 11,
        out_specs=[ANY, ANY],
    )
    return (outer[0], ends[0], ends[1], outer[1])


def solution(mesh):
    spec = P("ctx", "head")
    return jax.shard_map(
        per_device, mesh=mesh, in_specs=(spec,) * 5, out_specs=(spec,) * 4, check_vma=False
    )
```
